512 devices in a mesh: depth: 8 (over x_lo, y), azim: 64 (over z, x_hi, core).
Axes of the slice: x: 4 (x_hi: 2, x_lo: 2; x = x_hi * 2 + x_lo), y: 4, z: 16, core: 2. Of those that a mesh axis runs over, the one named last changes fastest.
Arguments:
- cotangent: bfloat16 [128, 4096, 256], P('depth', 'azim'), may hold values from -6 to 6
- pre_second: bfloat16 [128, 4096, 256], P('depth', 'azim'), may hold values from -6 to 6
- pre_first: bfloat16 [128, 4096, 256], P('depth', 'azim'), may hold values from -6 to 6
- kernel_first: bfloat16 [3, 3, 3, 32, 32], replicated, may hold values from -0.21875 to 0.21875
- kernel_second: bfloat16 [3, 3, 3, 32, 32], replicated, may hold values from -0.21875 to 0.21875
- row_resample: float32 [4, 128, 8, 8], P(None, 'depth'), may hold values from -0.1875 to 0.1875
- col_taps: float32 [4, 128, 8], P(None, 'depth'), may hold values from 0.1 to 1
- band_width: int32 [4, 128], P(None, 'depth'), may hold values from 1 to 8
- col_offset: int32 [4, 128], P(None, 'depth'), may hold values from -24 to 24, as said below
Outputs:
- cam_grad: float32 [8, 4096, 128], P('depth', 'azim')
The draws below stay inside these ranges and needn't reach their ends.
Inputs may be any that keep to these rules, and one draw needn't show every extreme that they name: `col_offset`: some entry equals -24 and some entry equals 24.
All inputs are finite; a program needn't handle non-finite values.
Results may differ from the reference program's by a relative error of at most 0.0048.
Values may be sent and summed in bfloat16 or wider, within the bound.
A program may use at most 64 MiB of HBM per device.

```python
import math
import jax
import jax.numpy as jnp
from jax import lax

C = 32
DEPTH = 128
AZIM = 4096
CAMS = 4
TAPS = 8
SHIFT = 24
ROWS = 8


def draw_col_offset(key, part):
    key_base, key_cam_low, key_sphere, key_cam_high = jax.random.split(jax.random.fold_in(key, 17), 4)
    offsets = jax.random.randint(key_base, (CAMS, DEPTH), -SHIFT, SHIFT + 1, dtype=jnp.int32)
    camera_low = jax.random.randint(key_cam_low, (), 0, CAMS, dtype=jnp.int32)
    sphere_low = jax.random.randint(key_sphere, (), 0, DEPTH, dtype=jnp.int32)
    camera_high = jax.random.randint(key_cam_high, (), 0, CAMS, dtype=jnp.int32)
    offsets = offsets.at[camera_low, sphere_low].set(-SHIFT)
    offsets = offsets.at[camera_high, (sphere_low + 1) % DEPTH].set(SHIFT)
    return offsets


def touch_ends(values, rng, low, largest):
    dims = values.shape
    place = [jax.random.randint(jax.random.fold_in(rng, axis), (), 0, dims[axis]) for axis in range(len(dims))]
    values = values.at[tuple(place)].set(low)
    longest = dims.index(max(dims))
    place[longest] = (place[longest] + 1) % dims[longest]
    return values.at[tuple(place)].set(largest)


def levels(stream_key, extent, pieces, least, top_value):
    level = 1.0
    for dim, blocks in pieces:
        heights = jax.random.uniform(jax.random.fold_in(jax.random.fold_in(stream_key, 6), dim), (blocks,), jnp.float32, least / len(pieces), top_value / len(pieces))
        level = level * jnp.repeat(jnp.exp(heights), extent[dim] // blocks).reshape((-1,) + (1,) * (len(extent) - 1 - dim))
    return level


def normal_values(own_key, shape, deviation, reach, shards=(), kind=jnp.bfloat16):
    gain = levels(own_key, shape, shards, -0.22, 0.18) if shards else 1.0
    entries = jax.random.normal(own_key, shape, jnp.float32) * deviation * gain
    return jnp.minimum(jnp.maximum(entries, -reach), reach).astype(kind)


def setup_inputs(seed: int = 0) -> dict:
    key_of = jax.random.split(jax.random.key(seed), 10)
    return {
        "cotangent": normal_values(key_of[0], (DEPTH, AZIM, ROWS * C), 1.0, 6.0, ((0, 8), (1, 64))),
        "pre_second": normal_values(key_of[1], (DEPTH, AZIM, ROWS * C), 1.0, 6.0, ((0, 8), (1, 64))),
        "pre_first": normal_values(key_of[2], (DEPTH, AZIM, ROWS * C), 1.0, 6.0, ((0, 8), (1, 64))),
        "kernel_first": normal_values(key_of[3], (3, 3, 3, C, C), (27 * C) ** -0.5, 0.21875),
        "kernel_second": normal_values(key_of[4], (3, 3, 3, C, C), (27 * C) ** -0.5, 0.21875),
        "row_resample": normal_values(key_of[5], (CAMS, DEPTH, ROWS, ROWS), (ROWS * DEPTH) ** -0.5, 0.1875, ((1, 8),), jnp.float32),
        "col_taps": jnp.clip(0.1 + 0.9 * jax.random.uniform(key_of[6], (CAMS, DEPTH, TAPS), jnp.float32) ** levels(key_of[6], (CAMS, DEPTH, TAPS), ((1, 8),), -0.2, 0.2), 0.1, 1.0),
        "band_width": touch_ends(jax.random.randint(key_of[7], (CAMS, DEPTH), 1, TAPS + 1), jax.random.fold_in(key_of[7], 1), 1, TAPS).astype(jnp.int32),
        "col_offset": draw_col_offset(jax.random.fold_in(key_of[9], 71), 0),
    }


def transpose_conv(grad, kernel):
    sphere_count, column_count, row_count, channels = grad.shape
    wrapped = jnp.concatenate([grad[:, -1:], grad, grad[:, :1]], axis=1)
    padded = jnp.pad(wrapped, ((1, 1), (0, 0), (1, 1), (0, 0)))
    flipped = jnp.transpose(kernel[::-1, ::-1, ::-1], (0, 1, 2, 4, 3)).astype(jnp.float32)
    blocksize = math.gcd(sphere_count, 8)

    def one_block(start):
        piece = lax.dynamic_slice_in_dim(padded, start, blocksize + 2, 0).astype(jnp.float32)
        result = lax.conv_general_dilated(piece[None], flipped, (1, 1, 1), "VALID",
                                          dimension_numbers=("NDHWC", "DHWIO", "NDHWC"),
                                          precision=lax.Precision.HIGHEST)
        return result[0]

    starts = jnp.arange(sphere_count // blocksize, dtype=jnp.int32) * blocksize
    return lax.map(one_block, starts).reshape(sphere_count, column_count, row_count, channels)


def reference(cotangent, pre_second, pre_first, kernel_first, kernel_second, row_resample, col_taps, band_width, col_offset):
    layout = (DEPTH, AZIM, ROWS, C)
    second_grad = jnp.where(pre_second > 0, cotangent, jnp.zeros_like(cotangent)).reshape(layout)
    hidden_grad = transpose_conv(second_grad, kernel_second)
    gate_first = (pre_first.reshape(layout) > 0).astype(jnp.float32)
    first_grad = (hidden_grad * gate_first).astype(jnp.bfloat16)
    volume_grad = transpose_conv(first_grad, kernel_first).astype(jnp.bfloat16)
    band_keep = lax.broadcasted_iota(jnp.int32, col_taps.shape, 2) < band_width[:, :, None]
    band_taps = jnp.where(band_keep, col_taps, jnp.zeros_like(col_taps)).astype(jnp.bfloat16)
    columns = jnp.arange(AZIM, dtype=jnp.int32)
    results = []
    for camera in range(CAMS):
        def step(accumulated, inputs):
            plane, taps_now, offset_now, resample = inputs
            pulled = jnp.zeros((AZIM, ROWS, C), jnp.float32)
            for tap in range(TAPS):
                source = ((columns + offset_now + tap) % AZIM).astype(jnp.int32)
                pulled = pulled + taps_now[tap].astype(jnp.float32) * jnp.take(plane, source, axis=0).astype(jnp.float32)
            accumulated = accumulated + jnp.einsum("hg,whc->gwc", resample, pulled, precision=lax.Precision.HIGHEST)
            return accumulated, None

        start = jnp.zeros((ROWS, AZIM, C), jnp.float32)
        accumulated, unused = lax.scan(step, start, (volume_grad, band_taps[camera], col_offset[camera], row_resample[camera]))
        results.append(accumulated)
    return jnp.concatenate(results, axis=-1)
```

```python
import numpy as np
import jax
import jax.numpy as jnp
from jax import lax
from jax.experimental import pallas as pl
from jax.experimental.pallas import tpu as pltpu
from jax.sharding import PartitionSpec as P

TAPS = 8
SHIFT = 24
NS = 16
NW = 64
ROWS = 8
C = 32
RC = ROWS * C
CAMS = 4
ND = 8
F32 = jnp.float32
BF16 = jnp.bfloat16
CH1 = 6
CH2 = 8


def stage_select():
    sel = np.zeros((160, 1024), np.float32)

    def at(array, sphere, column):
        part = 2 * array + (0 if column < 16 else 1)
        return 256 * part + 16 * sphere + column % 16

    for s in range(NS):
        sel[s, at(0, s, 62)] = 1
        sel[16 + s, at(0, s, 63)] = 1
        sel[32 + s, at(1, s, 63)] = 1
        sel[48 + s, at(0, s, 0)] = 1
        sel[64 + s, at(0, s, 1)] = 1
        sel[80 + s, at(1, s, 0)] = 1
    corners = ((96, 14, 62), (112, 14, 0), (128, 0, 62), (144, 0, 0))
    for base, sphere, column in corners:
        for i in range(4):
            sel[base + i, at(0, sphere + i // 2, column + i % 2)] = 1
        pf_sphere = 15 if sphere == 14 else 0
        pf_column = 63 if column == 62 else 0
        sel[base + 4, at(1, pf_sphere, pf_column)] = 1
    return sel


def edge_expand():
    mat = np.zeros((20 + 20 + 18, 16, 160), np.float32)
    for e in range(20):
        if e < 2:
            left, right = [96 + 2 * e, 97 + 2 * e], [112 + 2 * e, 113 + 2 * e]
        elif e < 18:
            left, right = [e - 2, 16 + e - 2], [48 + e - 2, 64 + e - 2]
        else:
            f = e - 18
            left, right = [128 + 2 * f, 129 + 2 * f], [144 + 2 * f, 145 + 2 * f]
        mat[e, 0, left[1]] = 1
        mat[e, 15, right[0]] = 1
        mat[20 + e, 0, left[0]] = 1
        mat[20 + e, 15, right[1]] = 1
    for f in range(18):
        left = 100 if f == 0 else 132 if f == 17 else 32 + f - 1
        right = 116 if f == 0 else 148 if f == 17 else 80 + f - 1
        mat[40 + f, 0, left] = 1
        mat[40 + f, 15, right] = 1
    return mat.reshape(-1, 160)


def row_place():
    place = np.zeros((ROWS, 3, C, ROWS, C), np.float32)
    for r_in in range(ROWS):
        for tap in range(3):
            r_out = r_in - 1 + tap
            if 0 <= r_out < ROWS:
                place[r_in, tap, np.arange(C), r_out, np.arange(C)] = 1
    return place.reshape(ROWS, 3 * C, RC)


def lane_rows():
    out = np.zeros((CAMS, ROWS, ROWS, RC), np.float32)
    lane = np.arange(RC)
    for k in range(CAMS):
        row = 4 * (lane // 128) + ((lane % 128) // 32 - k) % 4
        out[k, :, row, lane] = 1
    return out.reshape(CAMS, ROWS * ROWS, RC)


def sphere_lanes():
    out = np.zeros((NS, NS * NW), np.float32)
    out[np.arange(NS * NW) // NW, np.arange(NS * NW)] = 1
    return out


def kernel(
    cot_h, pre2_h, pre1_h, k1_h, k2_h, rr_h, taps_h, width_h, off_h,
    sel_h, exp_h, place_h, lrow_h, slane_h,
    out_ref,
    cot, pre2, pfx, g2x, kk, rr, taps, width, off,
    sel, expm, place, lrow, slane,
    stage, hc, s1, s2, pft, edges, kc, w2, w1, lbuf, rt, band, vol, ymix, zbuf, rbuf,
    in_sem, fs_sem, fr_sem, bs_sem, br_sem,
):
    d = lax.axis_index("depth")
    a = lax.axis_index("azim")
    na = lax.axis_size("azim")
    a_up = lax.rem(a + 1, na)
    a_dn = lax.rem(a + na - 1, na)

    def load(i, src, dst):
        copy = pltpu.make_async_copy(src, dst, in_sem.at[i])
        copy.start()
        return copy

    ld_pre1 = load(2, pre1_h, pfx.at[pl.ds(1, NS)])
    ld_cot = load(0, cot_h, cot)
    ld_pre2 = load(1, pre2_h, pre2)
    ld_sel = load(3, sel_h, sel)
    ld_k2 = load(4, k2_h, kk.at[0])
    ld_k1 = load(5, k1_h, kk.at[1])
    ld_place = load(6, place_h, place)
    ld_rr = load(7, rr_h, rr)
    ld_lrow = load(8, lrow_h, lrow)
    ld_taps = load(9, taps_h, taps)
    ld_width = load(10, width_h, width)
    ld_off = load(11, off_h, off)
    ld_slane = load(12, slane_h, slane)
    ld_exp = load(13, exp_h, expm)

    barrier = pltpu.get_barrier_semaphore()
    for j in range(ND):
        t = lax.rem(d + j, ND)
        for col in (a_dn, a, a_up):
            if j == 0 and col is a:
                continue
            pl.semaphore_signal(
                barrier, inc=1, device_id={"depth": t, "azim": col},
                device_id_type=pl.DeviceIdType.MESH,
            )

    @pl.when(d == 0)
    def _():
        g2x[0:2] = jnp.zeros((2, NW, RC), BF16)
        pfx[0:1] = jnp.zeros((1, NW, RC), BF16)
        hc[96:128] = jnp.zeros((32, RC), BF16)

    @pl.when(d == ND - 1)
    def _():
        g2x[18:20] = jnp.zeros((2, NW, RC), BF16)
        pfx[17:18] = jnp.zeros((1, NW, RC), BF16)
        hc[128:160] = jnp.zeros((32, RC), BF16)

    ld_cot.wait()
    ld_pre2.wait()
    g2x[2:18] = jnp.where(pre2[...] > 0, cot[...], jnp.zeros((), BF16))
    ld_pre1.wait()
    ld_sel.wait()
    acc = jnp.zeros((160, RC), F32)
    for part, ref in enumerate((g2x.at[2:18, 0:16], g2x.at[2:18, 48:64],
                                pfx.at[1:17, 0:16], pfx.at[1:17, 48:64])):
        acc = acc + jnp.dot(
            sel[:, 256 * part : 256 * part + 256], ref[...].reshape(256, RC),
            preferred_element_type=F32,
        )
    stage[...] = acc.astype(BF16)

    pl.semaphore_wait(barrier, 3 * ND - 1)

    def remote(i, src, dst, dep, col):
        return pltpu.make_async_remote_copy(
            src_ref=src, dst_ref=dst, send_sem=fs_sem.at[i], recv_sem=fr_sem.at[i],
            device_id={"depth": dep, "azim": col}, device_id_type=pl.DeviceIdType.MESH,
        )

    up = jnp.minimum(d + 1, ND - 1)
    dn = jnp.maximum(d - 1, 0)
    to_up = [
        remote(0, g2x.at[pl.ds(16, 2)], g2x.at[pl.ds(0, 2)], up, a),
        remote(1, pfx.at[pl.ds(16, 1)], pfx.at[pl.ds(0, 1)], up, a),
        remote(2, stage.at[pl.ds(96, 16)], hc.at[pl.ds(96, 16)], up, a_up),
        remote(3, stage.at[pl.ds(112, 16)], hc.at[pl.ds(112, 16)], up, a_dn),
    ]
    to_dn = [
        remote(4, g2x.at[pl.ds(2, 2)], g2x.at[pl.ds(18, 2)], dn, a),
        remote(5, pfx.at[pl.ds(1, 1)], pfx.at[pl.ds(17, 1)], dn, a),
        remote(6, stage.at[pl.ds(128, 16)], hc.at[pl.ds(128, 16)], dn, a_up),
        remote(7, stage.at[pl.ds(144, 16)], hc.at[pl.ds(144, 16)], dn, a_dn),
    ]
    sides = [
        remote(8, stage.at[pl.ds(0, 48)], hc.at[pl.ds(0, 48)], d, a_up),
        remote(9, stage.at[pl.ds(48, 48)], hc.at[pl.ds(48, 48)], d, a_dn),
    ]
    for copy in sides:
        copy.start()

    @pl.when(d < ND - 1)
    def _():
        for copy in to_up:
            copy.start()

    @pl.when(d > 0)
    def _():
        for copy in to_dn:
            copy.start()

    ld_k2.wait()
    ld_k1.wait()
    ld_place.wait()
    eye = (
        lax.broadcasted_iota(jnp.int32, (C, C), 0) == lax.broadcasted_iota(jnp.int32, (C, C), 1)
    ).astype(BF16)
    for layer, w in enumerate((w2, w1)):
        for pair in range(9):
            kc[layer, pl.ds(pair * C, C)] = lax.dot_general(
                eye, kk[layer, pair], (((1,), (1,)), ((), ())), preferred_element_type=F32
            ).astype(BF16)
        for r_in in range(ROWS):
            mixed = jnp.dot(kc[layer], place[r_in], preferred_element_type=F32)
            w[:, pl.ds(r_in * C, C), :] = mixed.astype(BF16).reshape(9, C, RC)

    ld_rr.wait()
    ld_lrow.wait()
    eye16 = (
        lax.broadcasted_iota(jnp.int32, (NS, NS), 0) == lax.broadcasted_iota(jnp.int32, (NS, NS), 1)
    ).astype(BF16)
    own_row = (
        lax.broadcasted_iota(jnp.int32, (ROWS * NS, ROWS * ROWS), 0) // NS
        == lax.broadcasted_iota(jnp.int32, (ROWS * NS, ROWS * ROWS), 1) // ROWS
    )
    for k in range(CAMS):
        turned = lax.dot_general(
            eye16, rr[k].astype(BF16), (((1,), (1,)), ((), ())), preferred_element_type=F32
        )
        picked = jnp.where(own_row, jnp.concatenate([turned] * ROWS, axis=0), 0.0)
        lbuf[pl.ds(k * NS * ROWS, NS * ROWS)] = jnp.dot(
            picked.astype(BF16), lrow[k], preferred_element_type=F32
        )
    chan_row = lax.broadcasted_iota(jnp.int32, (C, RC), 0)
    chan_lane = lax.rem(lax.broadcasted_iota(jnp.int32, (C, RC), 1), C)
    chan_same = (chan_row == chan_lane).astype(F32)

    def build_rt(i, carry):
        at = (i // NS) * (NS * ROWS) + lax.rem(i, NS)
        for r in range(ROWS):
            row = lbuf[pl.ds(at + r * NS, 1)]
            rt[i, r * C : (r + 1) * C] = (jnp.broadcast_to(row, (C, RC)) * chan_same).astype(BF16)
        return carry

    lax.fori_loop(0, CAMS * NS, build_rt, 0)

    ld_taps.wait()
    ld_width.wait()
    ld_off.wait()
    ld_slane.wait()
    lanes = NS * NW
    width_l = jnp.dot(width[...].astype(F32).astype(BF16), slane[...], preferred_element_type=F32)
    off_l = jnp.dot(off[...].astype(F32).astype(BF16), slane[...], preferred_element_type=F32)
    tap_index = lax.broadcasted_iota(jnp.int32, (TAPS, lanes), 0).astype(F32)
    u_lane = lax.rem(lax.broadcasted_iota(jnp.int32, (1, lanes), 1), NW).astype(F32)
    w_row = lax.broadcasted_iota(jnp.int32, (16, lanes), 0).astype(F32)
    for k in range(CAMS):
        taps_l = jnp.dot(taps[k].astype(BF16), slane[...], preferred_element_type=F32)
        taps_l = jnp.where(tap_index < width_l[k : k + 1], taps_l, 0.0)
        start = u_lane + 32.0 - off_l[k : k + 1]

        def build_band(block, carry):
            gap = start - (w_row + (block * 16).astype(F32))
            value = jnp.zeros((16, lanes), F32)
            for j in range(TAPS):
                value = jnp.where(gap == float(j), taps_l[j : j + 1], value)
            band[k, pl.ds(pl.multiple_of(block * 16, 16), 16)] = value.astype(BF16)
            return carry

        lax.fori_loop(0, 8, build_band, 0)

    ld_exp.wait()
    for copy in sides:
        copy.wait_recv()

    @pl.when(d < ND - 1)
    def _():
        for copy in to_dn:
            copy.wait_recv()

    @pl.when(d > 0)
    def _():
        for copy in to_up:
            copy.wait_recv()

    edges[...] = jnp.dot(expm[...], hc[...], preferred_element_type=F32)
    row16 = lax.broadcasted_iota(jnp.int32, (16, RC), 0)
    first = row16 == 0
    last = row16 == 15

    def build_s1(e, carry):
        x = g2x[e].astype(F32)
        near = edges[pl.ds(pl.multiple_of(e * 16, 16), 16)]
        far = edges[pl.ds(pl.multiple_of((20 + e) * 16, 16), 16)]
        ahead = pltpu.roll(x, NW - 1, 0)
        behind = pltpu.roll(x, 1, 0)
        s1[e, 0:48, 0:RC] = ahead[0:48].astype(BF16)
        s1[e, 48:64, 0:RC] = jnp.where(last, near, ahead[48:64]).astype(BF16)
        s1[e, 64:80, 0:RC] = jnp.where(first, x[0:16], far).astype(BF16)
        s1[e, 0:64, RC : 2 * RC] = g2x[e]
        s1[e, 64:80, RC : 2 * RC] = near.astype(BF16)
        s1[e, 0:16, 2 * RC :] = jnp.where(first, near, behind[0:16]).astype(BF16)
        s1[e, 16:64, 2 * RC :] = behind[16:64].astype(BF16)
        s1[e, 64:80, 2 * RC :] = jnp.where(last, x[48:64], far).astype(BF16)
        return carry

    lax.fori_loop(0, 20, build_s1, 0)

    def conv1(chunk, carry):
        base = chunk * CH1
        total = jnp.zeros((CH1 * 80, RC), F32)
        for td in range(3):
            total = total + jnp.dot(
                s1[pl.ds(base + 2 - td, CH1)].reshape(CH1 * 80, 3 * RC),
                w2[3 * td : 3 * td + 3].reshape(3 * RC, RC),
                preferred_element_type=F32,
            )
        for n in range(CH1):
            f = base + n
            x = jnp.where(pfx[f].astype(F32) > 0, total[n * 80 : n * 80 + 64], 0.0)
            gate = edges[pl.ds(pl.multiple_of((40 + f) * 16, 16), 16)]
            side = jnp.where(gate > 0, total[n * 80 + 64 : n * 80 + 80], 0.0)
            ahead = pltpu.roll(x, NW - 1, 0)
            behind = pltpu.roll(x, 1, 0)
            s2[f, 0:48, 0:RC] = ahead[0:48].astype(BF16)
            s2[f, 48:64, 0:RC] = jnp.where(last, side, ahead[48:64]).astype(BF16)
            s2[f, :, RC : 2 * RC] = x.astype(BF16)
            s2[f, 0:16, 2 * RC :] = jnp.where(first, side, behind[0:16]).astype(BF16)
            s2[f, 16:64, 2 * RC :] = behind[16:64].astype(BF16)
        return carry

    lax.fori_loop(0, 18 // CH1, conv1, 0)

    def conv2(chunk, carry):
        base = chunk * CH2
        total = jnp.zeros((CH2 * NW, RC), F32)
        for td in range(3):
            total = total + jnp.dot(
                s2[pl.ds(base + 2 - td, CH2)].reshape(CH2 * NW, 3 * RC),
                w1[3 * td : 3 * td + 3].reshape(3 * RC, RC),
                preferred_element_type=F32,
            )
        vol[pl.ds(base, CH2)] = total.astype(BF16).reshape(CH2, NW, RC)
        return carry

    lax.fori_loop(0, NS // CH2, conv2, 0)

    def mix(s, carry):
        v = vol[s]
        for k in range(CAMS):
            ymix[k, s] = jnp.dot(v, rt[k * NS + s], preferred_element_type=F32).astype(BF16)
        return carry

    lax.fori_loop(0, NS, mix, 0)

    cams = [
        jnp.dot(band[k], ymix[k].reshape(NS * NW, RC), preferred_element_type=F32)
        for k in range(CAMS)
    ]
    block = lax.broadcasted_iota(jnp.int32, (128, 128), 1) // C
    for r2 in range(ROWS):
        half, turn = r2 // 4, r2 % 4
        parts = [cams[(b - turn) % 4][:, half * 128 : half * 128 + 128] for b in range(4)]
        z = jnp.where(
            block < 2,
            jnp.where(block == 0, parts[0], parts[1]),
            jnp.where(block == 2, parts[2], parts[3]),
        )
        zbuf[r2] = z.astype(BF16)

    def back(i, j, src_row, rows, dst_row, col):
        t = lax.rem(d + j, ND)
        return pltpu.make_async_remote_copy(
            src_ref=zbuf.at[t, pl.ds(src_row, rows)],
            dst_ref=rbuf.at[j, pl.ds(dst_row, rows)],
            send_sem=bs_sem.at[i, j], recv_sem=br_sem.at[i, j],
            device_id={"depth": t, "azim": col}, device_id_type=pl.DeviceIdType.MESH,
        )

    copies = []
    for j in list(range(1, ND)) + [0]:
        if j:
            copies.append(back(0, j, 32, 64, 0, a))
        copies.append(back(1, j, 96, 32, 64, a_up))
        copies.append(back(2, j, 0, 32, 96, a_dn))
    for copy in copies:
        copy.start()
    rbuf[0, 0:64] = zbuf[d, 32:96]

    for copy in copies:
        copy.wait_recv()
    total = jnp.zeros((NW, 128), F32)
    for j in range(ND):
        total = total + (rbuf[j, 0:64].astype(F32) + rbuf[j, 64:128].astype(F32))
    turn = lax.rem(d, 4)
    out_ref[0] = pltpu.roll(total, lax.rem(4 - turn, 4) * C, 1)

    for copy in copies:
        copy.wait_send()
    for copy in sides:
        copy.wait_send()

    @pl.when(d < ND - 1)
    def _():
        for copy in to_up:
            copy.wait_send()

    @pl.when(d > 0)
    def _():
        for copy in to_dn:
            copy.wait_send()


def body(cotangent, pre_second, pre_first, kernel_first, kernel_second, row_resample, col_taps, band_width, col_offset):
    consts = [
        jnp.asarray(x, BF16)
        for x in (stage_select(), edge_expand(), row_place(), lane_rows(), sphere_lanes())
    ]
    vm = pltpu.VMEM
    scratch = [
        vm((NS, NW, RC), BF16), vm((NS, NW, RC), BF16), vm((18, NW, RC), BF16),
        vm((20, NW, RC), BF16), vm((2, 9, 96, C), BF16), vm((CAMS, ROWS * ROWS, NS), F32),
        vm((CAMS, TAPS, NS), F32), vm((CAMS, NS), jnp.int32), vm((CAMS, NS), jnp.int32),
        vm((160, 1024), BF16), vm((58 * 16, 160), BF16), vm((ROWS, 96, RC), BF16),
        vm((CAMS, ROWS * ROWS, RC), BF16), vm((NS, NS * NW), BF16),
        vm((160, RC), BF16), vm((160, RC), BF16),
        vm((20, 80, 3 * RC), BF16), vm((18, NW, 3 * RC), BF16), vm((16, RC), F32),
        vm((58 * 16, RC), F32), vm((2, 288, 96), BF16),
        vm((9, RC, RC), BF16), vm((9, RC, RC), BF16),
        vm((CAMS * NS * ROWS, RC), F32), vm((CAMS * NS, RC, RC), BF16),
        vm((CAMS, 128, NS * NW), BF16), vm((NS, NW, RC), BF16), vm((CAMS, NS, NW, RC), BF16),
        vm((ROWS, 128, 128), BF16), vm((ND, 128, 128), BF16),
        pltpu.SemaphoreType.DMA((14,)), pltpu.SemaphoreType.DMA((10,)),
        pltpu.SemaphoreType.DMA((10,)), pltpu.SemaphoreType.DMA((3, ND)),
        pltpu.SemaphoreType.DMA((3, ND)),
    ]
    return pl.pallas_call(
        kernel,
        out_shape=jax.ShapeDtypeStruct((1, NW, 128), F32),
        in_specs=[pl.BlockSpec(memory_space=pl.ANY)] * 14,
        out_specs=pl.BlockSpec(memory_space=pltpu.VMEM),
        scratch_shapes=scratch,
        compiler_params=pltpu.CompilerParams(
            collective_id=0, has_side_effects=True, vmem_limit_bytes=62 * 1024 * 1024
        ),
    )(
        cotangent, pre_second, pre_first,
        kernel_first.reshape(9, 96, C), kernel_second.reshape(9, 96, C),
        row_resample.transpose(0, 2, 3, 1).reshape(CAMS, ROWS * ROWS, NS), col_taps.transpose(0, 2, 1),
        band_width, col_offset, *consts,
    )


def solution(mesh):
    placed = (
        P("depth", "azim", None),
        P("depth", "azim", None),
        P("depth", "azim", None),
        P(),
        P(),
        P(None, "depth", None, None),
        P(None, "depth", None),
        P(None, "depth"),
        P(None, "depth"),
    )
    return jax.shard_map(
        body, mesh=mesh, in_specs=placed, out_specs=P("depth", "azim", None), check_vma=False
    )
```

```python
import numpy as np
import jax
import jax.numpy as jnp
from jax import lax
from jax.experimental import pallas as pl
from jax.experimental.pallas import tpu as pltpu
from jax.sharding import PartitionSpec as P

TAPS = 8
SHIFT = 24
NS = 16
NW = 64
ROWS = 8
C = 32
RC = ROWS * C
CAMS = 4
ND = 8
F32 = jnp.float32
BF16 = jnp.bfloat16
CH1 = 6
CH2 = 8


def stage_select():
    sel = np.zeros((160, 1024), np.float32)

    def at(array, sphere, column):
        part = 2 * array + (0 if column < 16 else 1)
        return 256 * part + 16 * sphere + column % 16

    for s in range(NS):
        sel[s, at(0, s, 62)] = 1
        sel[16 + s, at(0, s, 63)] = 1
        sel[32 + s, at(1, s, 63)] = 1
        sel[48 + s, at(0, s, 0)] = 1
        sel[64 + s, at(0, s, 1)] = 1
        sel[80 + s, at(1, s, 0)] = 1
    corners = ((96, 14, 62), (112, 14, 0), (128, 0, 62), (144, 0, 0))
    for base, sphere, column in corners:
        for i in range(4):
            sel[base + i, at(0, sphere + i // 2, column + i % 2)] = 1
        pf_sphere = 15 if sphere == 14 else 0
        pf_column = 63 if column == 62 else 0
        sel[base + 4, at(1, pf_sphere, pf_column)] = 1
    return sel


def edge_expand():
    mat = np.zeros((20 + 20 + 18, 16, 160), np.float32)
    for e in range(20):
        if e < 2:
            left, right = [96 + 2 * e, 97 + 2 * e], [112 + 2 * e, 113 + 2 * e]
        elif e < 18:
            left, right = [e - 2, 16 + e - 2], [48 + e - 2, 64 + e - 2]
        else:
            f = e - 18
            left, right = [128 + 2 * f, 129 + 2 * f], [144 + 2 * f, 145 + 2 * f]
        mat[e, 0, left[1]] = 1
        mat[e, 15, right[0]] = 1
        mat[20 + e, 0, left[0]] = 1
        mat[20 + e, 15, right[1]] = 1
    for f in range(18):
        left = 100 if f == 0 else 132 if f == 17 else 32 + f - 1
        right = 116 if f == 0 else 148 if f == 17 else 80 + f - 1
        mat[40 + f, 0, left] = 1
        mat[40 + f, 15, right] = 1
    return mat.reshape(-1, 160)


def row_place():
    place = np.zeros((2, ROWS, 3, C, RC), np.float32)
    i = np.arange(C)
    for r_in in range(ROWS):
        for tap in range(3):
            r_out = r_in - 1 + tap
            if 0 <= r_out < ROWS:
                place[0, r_in, tap, i, r_out * C + i] = 1
                place[1, r_in, tap, i, (i // 16) * 128 + r_out * 16 + i % 16] = 1
    return place.reshape(2, ROWS, 3 * C, RC)


def lane_rows():
    out = np.zeros((CAMS, ROWS, ROWS, 128), np.float32)
    lane = np.arange(128)
    for k in range(CAMS):
        out[k, :, (lane // 16 - 2 * k) % 8, lane] = 1
    return out.reshape(CAMS, ROWS * ROWS, 128)


def sphere_lanes():
    out = np.zeros((NS, NS * NW), np.float32)
    out[np.arange(NS * NW) // NW, np.arange(NS * NW)] = 1
    return out


def kernel(
    cot_h, pre2_h, pre1_h, k1_h, k2_h, rr_h, taps_h, width_h, off_h,
    sel_h, exp_h, place_h, lrow_h, slane_h,
    out_ref,
    cot, pre2, pfx, g2x, kk, rr, taps, width, off,
    sel, expm, place, lrow, slane,
    stage, hc, s1, s2, pft, edges, kc, w2, w1, lbuf, rt, band, vol, ymix, zbuf, rbuf,
    in_sem, fs_sem, fr_sem, bs_sem, br_sem,
):
    d = lax.axis_index("depth")
    a = lax.axis_index("azim")
    na = lax.axis_size("azim")
    a_up = lax.rem(a + 1, na)
    a_dn = lax.rem(a + na - 1, na)

    def load(i, src, dst):
        copy = pltpu.make_async_copy(src, dst, in_sem.at[i])
        copy.start()
        return copy

    ld_pre1 = load(2, pre1_h, pfx.at[pl.ds(1, NS)])
    ld_cot = load(0, cot_h, cot)
    ld_pre2 = load(1, pre2_h, pre2)
    ld_sel = load(3, sel_h, sel)
    ld_k2 = load(4, k2_h, kk.at[0])
    ld_k1 = load(5, k1_h, kk.at[1])
    ld_place = load(6, place_h, place)
    ld_rr = load(7, rr_h, rr)
    ld_lrow = load(8, lrow_h, lrow)
    ld_taps = load(9, taps_h, taps)
    ld_width = load(10, width_h, width)
    ld_off = load(11, off_h, off)
    ld_slane = load(12, slane_h, slane)
    ld_exp = load(13, exp_h, expm)

    barrier = pltpu.get_barrier_semaphore()
    for j in range(ND):
        t = lax.rem(d + j, ND)
        for col in (a_dn, a, a_up):
            if j == 0 and col is a:
                continue
            pl.semaphore_signal(
                barrier, inc=1, device_id={"depth": t, "azim": col},
                device_id_type=pl.DeviceIdType.MESH,
            )

    @pl.when(d == 0)
    def _():
        g2x[0:2] = jnp.zeros((2, NW, RC), BF16)
        pfx[0:1] = jnp.zeros((1, NW, RC), BF16)
        hc[96:128] = jnp.zeros((32, RC), BF16)

    @pl.when(d == ND - 1)
    def _():
        g2x[18:20] = jnp.zeros((2, NW, RC), BF16)
        pfx[17:18] = jnp.zeros((1, NW, RC), BF16)
        hc[128:160] = jnp.zeros((32, RC), BF16)

    ld_cot.wait()
    ld_pre2.wait()
    g2x[2:18] = jnp.where(pre2[...] > 0, cot[...], jnp.zeros((), BF16))
    ld_pre1.wait()
    ld_sel.wait()
    acc = jnp.zeros((160, RC), F32)
    for part, ref in enumerate((g2x.at[2:18, 0:16], g2x.at[2:18, 48:64],
                                pfx.at[1:17, 0:16], pfx.at[1:17, 48:64])):
        acc = acc + jnp.dot(
            sel[:, 256 * part : 256 * part + 256], ref[...].reshape(256, RC),
            preferred_element_type=F32,
        )
    stage[...] = acc.astype(BF16)

    pl.semaphore_wait(barrier, 3 * ND - 1)

    def remote(group, src, dst, dep, col):
        return pltpu.make_async_remote_copy(
            src_ref=src, dst_ref=dst, send_sem=fs_sem.at[group], recv_sem=fr_sem.at[group],
            device_id={"depth": dep, "azim": col}, device_id_type=pl.DeviceIdType.MESH,
        )

    up = jnp.minimum(d + 1, ND - 1)
    dn = jnp.maximum(d - 1, 0)
    to_up = [
        remote(1, g2x.at[pl.ds(16, 2)], g2x.at[pl.ds(0, 2)], up, a),
        remote(1, pfx.at[pl.ds(16, 1)], pfx.at[pl.ds(0, 1)], up, a),
        remote(1, stage.at[pl.ds(96, 16)], hc.at[pl.ds(96, 16)], up, a_up),
        remote(1, stage.at[pl.ds(112, 16)], hc.at[pl.ds(112, 16)], up, a_dn),
    ]
    to_dn = [
        remote(2, g2x.at[pl.ds(2, 2)], g2x.at[pl.ds(18, 2)], dn, a),
        remote(2, pfx.at[pl.ds(1, 1)], pfx.at[pl.ds(17, 1)], dn, a),
        remote(2, stage.at[pl.ds(128, 16)], hc.at[pl.ds(128, 16)], dn, a_up),
        remote(2, stage.at[pl.ds(144, 16)], hc.at[pl.ds(144, 16)], dn, a_dn),
    ]
    sides = [
        remote(0, stage.at[pl.ds(0, 48)], hc.at[pl.ds(0, 48)], d, a_up),
        remote(0, stage.at[pl.ds(48, 48)], hc.at[pl.ds(48, 48)], d, a_dn),
    ]
    for copy in sides:
        copy.start()

    @pl.when(d < ND - 1)
    def _():
        for copy in to_up:
            copy.start()

    @pl.when(d > 0)
    def _():
        for copy in to_dn:
            copy.start()

    def drain(sem, rows):
        view = w2.at[0, pl.ds(0, rows)]
        pltpu.make_async_copy(view, view, sem).wait()

    ld_k2.wait()
    ld_k1.wait()
    ld_place.wait()
    eye = (
        lax.broadcasted_iota(jnp.int32, (C, C), 0) == lax.broadcasted_iota(jnp.int32, (C, C), 1)
    ).astype(BF16)
    for layer, w in enumerate((w2, w1)):
        for pair in range(9):
            kc[layer, pl.ds(pair * C, C)] = lax.dot_general(
                eye, kk[layer, pair], (((1,), (1,)), ((), ())), preferred_element_type=F32
            ).astype(BF16)
        for r_in in range(ROWS):
            mixed = jnp.dot(kc[layer], place[layer, r_in], preferred_element_type=F32)
            w[:, pl.ds(r_in * C, C), :] = mixed.astype(BF16).reshape(9, C, RC)

    ld_rr.wait()
    ld_lrow.wait()
    eye16 = (
        lax.broadcasted_iota(jnp.int32, (NS, NS), 0) == lax.broadcasted_iota(jnp.int32, (NS, NS), 1)
    ).astype(BF16)
    own_row = (
        lax.broadcasted_iota(jnp.int32, (ROWS * NS, ROWS * ROWS), 0) // NS
        == lax.broadcasted_iota(jnp.int32, (ROWS * NS, ROWS * ROWS), 1) // ROWS
    )
    for k in range(CAMS):
        turned = lax.dot_general(
            eye16, rr[k].astype(BF16), (((1,), (1,)), ((), ())), preferred_element_type=F32
        )
        picked = jnp.where(own_row, jnp.concatenate([turned] * ROWS, axis=0), 0.0)
        lbuf[pl.ds(k * NS * ROWS, NS * ROWS)] = jnp.dot(
            picked.astype(BF16), lrow[k], preferred_element_type=F32
        )
    chan_row = lax.broadcasted_iota(jnp.int32, (16, 128), 0)
    chan_lane = lax.rem(lax.broadcasted_iota(jnp.int32, (16, 128), 1), 16)
    chan_same = (chan_row == chan_lane).astype(F32)

    def build_rt(s, carry):
        for k in range(CAMS):
            for r in range(ROWS):
                row = lbuf[pl.ds((k * ROWS + r) * NS + s, 1)]
                rt[s, r * 16 : (r + 1) * 16, k * 128 : (k + 1) * 128] = (
                    jnp.broadcast_to(row, (16, 128)) * chan_same
                ).astype(BF16)
        return carry

    lax.fori_loop(0, NS, build_rt, 0)

    ld_taps.wait()
    ld_width.wait()
    ld_off.wait()
    ld_slane.wait()
    lanes = NS * NW
    width_l = jnp.dot(width[...].astype(F32).astype(BF16), slane[...], preferred_element_type=F32)
    off_l = jnp.dot(off[...].astype(F32).astype(BF16), slane[...], preferred_element_type=F32)
    tap_index = lax.broadcasted_iota(jnp.int32, (TAPS, lanes), 0).astype(F32)
    u_lane = lax.rem(lax.broadcasted_iota(jnp.int32, (1, lanes), 1), NW).astype(F32)
    w_row = lax.broadcasted_iota(jnp.int32, (16, lanes), 0).astype(F32).astype(BF16)
    for k in range(CAMS):
        taps_l = jnp.dot(taps[k].astype(BF16), slane[...], preferred_element_type=F32)
        taps_l = jnp.where(tap_index < width_l[k : k + 1], taps_l, 0.0)
        wide = [
            jnp.broadcast_to(taps_l[j : j + 1], (16, lanes)).astype(BF16) for j in range(TAPS)
        ]
        start = jnp.broadcast_to(u_lane + 32.0 - off_l[k : k + 1], (16, lanes)).astype(BF16) - w_row

        def build_band(block, carry):
            gap = start - (block * 16).astype(F32).astype(BF16)
            value = jnp.zeros((16, lanes), BF16)
            for j in range(TAPS):
                value = jnp.where(gap == jnp.asarray(j, BF16), wide[j], value)
            band[k, pl.ds(pl.multiple_of(block * 16, 16), 16)] = value
            return carry

        lax.fori_loop(0, 8, build_band, 0)

    ld_exp.wait()
    drain(fr_sem.at[0], 96)

    @pl.when(d < ND - 1)
    def _():
        drain(fr_sem.at[2], 224)

    @pl.when(d > 0)
    def _():
        drain(fr_sem.at[1], 224)

    edges[...] = jnp.dot(expm[...], hc[...], preferred_element_type=F32)
    row16 = lax.broadcasted_iota(jnp.int32, (16, RC), 0)
    first = row16 == 0
    last = row16 == 15

    def build_s1(e, carry):
        x = g2x[e].astype(F32)
        near = edges[pl.ds(pl.multiple_of(e * 16, 16), 16)]
        far = edges[pl.ds(pl.multiple_of((20 + e) * 16, 16), 16)]
        ahead = pltpu.roll(x, NW - 1, 0)
        behind = pltpu.roll(x, 1, 0)
        s1[e, 0:48, 0:RC] = ahead[0:48].astype(BF16)
        s1[e, 48:64, 0:RC] = jnp.where(last, near, ahead[48:64]).astype(BF16)
        s1[e, 64:80, 0:RC] = jnp.where(first, x[0:16], far).astype(BF16)
        s1[e, 0:64, RC : 2 * RC] = g2x[e]
        s1[e, 64:80, RC : 2 * RC] = near.astype(BF16)
        s1[e, 0:16, 2 * RC :] = jnp.where(first, near, behind[0:16]).astype(BF16)
        s1[e, 16:64, 2 * RC :] = behind[16:64].astype(BF16)
        s1[e, 64:80, 2 * RC :] = jnp.where(last, x[48:64], far).astype(BF16)
        return carry

    lax.fori_loop(0, 20, build_s1, 0)

    def conv1(chunk, carry):
        base = chunk * CH1
        total = jnp.zeros((CH1 * 80, RC), F32)
        for td in range(3):
            total = total + jnp.dot(
                s1[pl.ds(base + 2 - td, CH1)].reshape(CH1 * 80, 3 * RC),
                w2[3 * td : 3 * td + 3].reshape(3 * RC, RC),
                preferred_element_type=F32,
            )
        for n in range(CH1):
            f = base + n
            x = jnp.where(pfx[f].astype(F32) > 0, total[n * 80 : n * 80 + 64], 0.0)
            gate = edges[pl.ds(pl.multiple_of((40 + f) * 16, 16), 16)]
            side = jnp.where(gate > 0, total[n * 80 + 64 : n * 80 + 80], 0.0)
            ahead = pltpu.roll(x, NW - 1, 0)
            behind = pltpu.roll(x, 1, 0)
            s2[f, 0:48, 0:RC] = ahead[0:48].astype(BF16)
            s2[f, 48:64, 0:RC] = jnp.where(last, side, ahead[48:64]).astype(BF16)
            s2[f, :, RC : 2 * RC] = x.astype(BF16)
            s2[f, 0:16, 2 * RC :] = jnp.where(first, side, behind[0:16]).astype(BF16)
            s2[f, 16:64, 2 * RC :] = behind[16:64].astype(BF16)
        return carry

    lax.fori_loop(0, 18 // CH1, conv1, 0)

    def conv2(chunk, carry):
        base = chunk * CH2
        total = jnp.zeros((CH2 * NW, RC), F32)
        for td in range(3):
            total = total + jnp.dot(
                s2[pl.ds(base + 2 - td, CH2)].reshape(CH2 * NW, 3 * RC),
                w1[3 * td : 3 * td + 3].reshape(3 * RC, RC),
                preferred_element_type=F32,
            )
        vol[pl.ds(base, CH2)] = total.astype(BF16).reshape(CH2, NW, RC)
        return carry

    lax.fori_loop(0, NS // CH2, conv2, 0, unroll=True)

    def mix(s, carry):
        v = jnp.concatenate([vol[s, :, 0:128], vol[s, :, 128:256]], axis=0)
        y = jnp.dot(v, rt[s], preferred_element_type=F32).astype(BF16)
        for k in range(CAMS):
            ymix[k, s, :, 0:128] = y[0:64, k * 128 : k * 128 + 128]
            ymix[k, s, :, 128:256] = y[64:128, k * 128 : k * 128 + 128]
        return carry

    lax.fori_loop(0, NS, mix, 0, unroll=True)

    source = []
    for k in range(CAMS):
        cam = jnp.dot(band[k], ymix[k].reshape(NS * NW, RC), preferred_element_type=F32)
        source.append(cam[:, 0:128].astype(BF16))
        source.append(pltpu.roll(cam[:, 128:256], 16, 1).astype(BF16))
    block = lax.broadcasted_iota(jnp.int32, (128, 128), 1) // 16
    for r2 in range(ROWS):
        z = source[0]
        for q in range(1, ROWS):
            z = jnp.where(block == (r2 + q) % 8, source[q], z)
        zbuf[r2] = z

    def back(j, src_row, rows, dst_row, col):
        t = lax.rem(d + j, ND)
        return pltpu.make_async_remote_copy(
            src_ref=zbuf.at[t, pl.ds(src_row, rows)],
            dst_ref=rbuf.at[pl.ds(j * 128 + dst_row, rows)],
            send_sem=bs_sem, recv_sem=br_sem,
            device_id={"depth": t, "azim": col}, device_id_type=pl.DeviceIdType.MESH,
        )

    for j in list(range(1, ND)) + [0]:
        if j:
            back(j, 32, 64, 0, a).start()
        back(j, 96, 32, 64, a_up).start()
        back(j, 0, 32, 96, a_dn).start()
    rbuf[0:64] = zbuf[d, 32:96]

    arrived = rbuf.at[pl.ds(64, ND * 128 - 64)]
    pltpu.make_async_copy(arrived, arrived, br_sem).wait()
    total = jnp.zeros((NW, 128), F32)
    for j in range(ND):
        own = rbuf[j * 128 : j * 128 + 64].astype(F32)
        total = total + (own + rbuf[j * 128 + 64 : j * 128 + 128].astype(F32))
    out_ref[0] = pltpu.roll(total, lax.rem(ND - d, ND) * 16, 1)

    pltpu.make_async_copy(arrived, arrived, bs_sem).wait()
    drain(fs_sem.at[0], 96)

    @pl.when(d < ND - 1)
    def _():
        drain(fs_sem.at[1], 224)

    @pl.when(d > 0)
    def _():
        drain(fs_sem.at[2], 224)


def body(cotangent, pre_second, pre_first, kernel_first, kernel_second, row_resample, col_taps, band_width, col_offset):
    consts = [
        jnp.asarray(x, BF16)
        for x in (stage_select(), edge_expand(), row_place(), lane_rows(), sphere_lanes())
    ]
    vm = pltpu.VMEM
    scratch = [
        vm((NS, NW, RC), BF16), vm((NS, NW, RC), BF16), vm((18, NW, RC), BF16),
        vm((20, NW, RC), BF16), vm((2, 9, 96, C), BF16), vm((CAMS, ROWS * ROWS, NS), F32),
        vm((CAMS, TAPS, NS), F32), vm((CAMS, NS), jnp.int32), vm((CAMS, NS), jnp.int32),
        vm((160, 1024), BF16), vm((58 * 16, 160), BF16), vm((2, ROWS, 96, RC), BF16),
        vm((CAMS, ROWS * ROWS, 128), BF16), vm((NS, NS * NW), BF16),
        vm((160, RC), BF16), vm((160, RC), BF16),
        vm((20, 80, 3 * RC), BF16), vm((18, NW, 3 * RC), BF16), vm((16, RC), F32),
        vm((58 * 16, RC), F32), vm((2, 288, 96), BF16),
        vm((9, RC, RC), BF16), vm((9, RC, RC), BF16),
        vm((CAMS * NS * ROWS, 128), F32), vm((NS, 128, CAMS * 128), BF16),
        vm((CAMS, 128, NS * NW), BF16), vm((NS, NW, RC), BF16), vm((CAMS, NS, NW, RC), BF16),
        vm((ROWS, 128, 128), BF16), vm((ND * 128, 128), BF16),
        pltpu.SemaphoreType.DMA((14,)), pltpu.SemaphoreType.DMA((3,)),
        pltpu.SemaphoreType.DMA((3,)), pltpu.SemaphoreType.DMA, pltpu.SemaphoreType.DMA,
    ]
    return pl.pallas_call(
        kernel,
        out_shape=jax.ShapeDtypeStruct((1, NW, 128), F32),
        in_specs=[pl.BlockSpec(memory_space=pl.ANY)] * 14,
        out_specs=pl.BlockSpec(memory_space=pltpu.VMEM),
        scratch_shapes=scratch,
        compiler_params=pltpu.CompilerParams(
            collective_id=0, has_side_effects=True, vmem_limit_bytes=62 * 1024 * 1024
        ),
    )(
        cotangent, pre_second, pre_first,
        kernel_first.reshape(9, 96, C), kernel_second.reshape(9, 96, C),
        row_resample.transpose(0, 2, 3, 1).reshape(CAMS, ROWS * ROWS, NS), col_taps.transpose(0, 2, 1),
        band_width, col_offset, *consts,
    )


def solution(mesh):
    placed = (
        P("depth", "azim", None),
        P("depth", "azim", None),
        P("depth", "azim", None),
        P(),
        P(),
        P(None, "depth", None, None),
        P(None, "depth", None),
        P(None, "depth"),
        P(None, "depth"),
    )
    return jax.shard_map(
        body, mesh=mesh, in_specs=placed, out_specs=P("depth", "azim", None), check_vma=False
    )
```

```python
import numpy as np
import jax
import jax.numpy as jnp
from jax import lax
from jax.experimental import pallas as pl
from jax.experimental.pallas import tpu as pltpu
from jax.sharding import PartitionSpec as P

TAPS = 8
SHIFT = 24
NS = 16
NW = 64
ROWS = 8
C = 32
RC = ROWS * C
CAMS = 4
ND = 8
F32 = jnp.float32
BF16 = jnp.bfloat16
EARLYB = 1
EARLYR = 0
EARLYW = 0
US2 = 3
CH1 = 7
CH2 = 8


def stage_select():
    sel = np.zeros((160, 1024), np.float32)

    def at(array, sphere, column):
        part = 2 * array + (0 if column < 16 else 1)
        return 256 * part + 16 * sphere + column % 16

    for s in range(NS):
        sel[s, at(0, s, 62)] = 1
        sel[16 + s, at(0, s, 63)] = 1
        sel[32 + s, at(1, s, 63)] = 1
        sel[48 + s, at(0, s, 0)] = 1
        sel[64 + s, at(0, s, 1)] = 1
        sel[80 + s, at(1, s, 0)] = 1
    corners = ((96, 14, 62), (112, 14, 0), (128, 0, 62), (144, 0, 0))
    for base, sphere, column in corners:
        for i in range(4):
            sel[base + i, at(0, sphere + i // 2, column + i % 2)] = 1
        pf_sphere = 15 if sphere == 14 else 0
        pf_column = 63 if column == 62 else 0
        sel[base + 4, at(1, pf_sphere, pf_column)] = 1
    return sel


def edge_expand():
    mat = np.zeros((3 * 20 + 18, 16, 160), np.float32)
    for e in range(20):
        if e < 2:
            left, right = [96 + 2 * e, 97 + 2 * e], [112 + 2 * e, 113 + 2 * e]
        elif e < 18:
            left, right = [e - 2, 16 + e - 2], [48 + e - 2, 64 + e - 2]
        else:
            f = e - 18
            left, right = [128 + 2 * f, 129 + 2 * f], [144 + 2 * f, 145 + 2 * f]
        mat[e, 14, right[1]] = 1
        mat[e, 15, right[0]] = 1
        mat[20 + e, 1, left[1]] = 1
        mat[20 + e, 14, right[0]] = 1
        mat[40 + e, 0, left[1]] = 1
        mat[40 + e, 1, left[0]] = 1
    for f in range(18):
        left = 100 if f == 0 else 132 if f == 17 else 32 + f - 1
        right = 116 if f == 0 else 148 if f == 17 else 80 + f - 1
        mat[60 + f, 1, left] = 1
        mat[60 + f, 14, right] = 1
    return mat.reshape(-1, 160)


def row_place():
    place = np.zeros((2, ROWS, 3, C, RC), np.float32)
    i = np.arange(C)
    for r_in in range(ROWS):
        for tap in range(3):
            r_out = r_in - 1 + tap
            if 0 <= r_out < ROWS:
                place[0, r_in, tap, i, r_out * C + i] = 1
                place[1, r_in, tap, i, (i // 16) * 128 + r_out * 16 + i % 16] = 1
    return place.reshape(2, ROWS, 3 * C, RC)


def lane_rows():
    out = np.zeros((CAMS, ROWS, ROWS, 128), np.float32)
    lane = np.arange(128)
    for k in range(CAMS):
        out[k, :, (lane // 16 - 2 * k) % 8, lane] = 1
    return out.reshape(CAMS, ROWS * ROWS, 128)


def sphere_lanes():
    out = np.zeros((NS, NS * NW), np.float32)
    out[np.arange(NS * NW) // NW, np.arange(NS * NW)] = 1
    return out


def kernel(
    cot_h, pre2_h, pre1_h, k1_h, k2_h, rr_h, taps_h, width_h, off_h,
    sel_h, exp_h, place_h, lrow_h, slane_h,
    out_ref,
    cot, pre2, pfx, g2x, kk, rr, taps, width, off,
    sel, expm, place, lrow, slane,
    stage, hc, s1, t1, s2, hidden, fix, edges, kc, w2, w1, lbuf, rt, band, vol, ymix, zbuf, rbuf,
    in_sem, fs_sem, fr_sem, bs_sem, br_sem,
):
    d = lax.axis_index("depth")
    a = lax.axis_index("azim")
    na = lax.axis_size("azim")
    a_up = lax.rem(a + 1, na)
    a_dn = lax.rem(a + na - 1, na)

    def load(i, src, dst):
        copy = pltpu.make_async_copy(src, dst, in_sem.at[i])
        copy.start()
        return copy

    ld_cot = load(0, cot_h, cot)
    ld_pre2 = load(1, pre2_h, pre2)
    ld_taps = load(9, taps_h, taps)
    ld_width = load(10, width_h, width)
    ld_off = load(11, off_h, off)
    ld_slane = load(12, slane_h, slane)
    ld_pre1 = load(2, pre1_h, pfx.at[pl.ds(1, NS)])
    ld_sel = load(3, sel_h, sel)

    barrier = pltpu.get_barrier_semaphore()
    for j in range(ND):
        t = lax.rem(d + j, ND)
        for col in (a_dn, a, a_up):
            if j == 0 and col is a:
                continue
            pl.semaphore_signal(
                barrier, inc=1, device_id={"depth": t, "azim": col},
                device_id_type=pl.DeviceIdType.MESH,
            )

    ld_rr = load(7, rr_h, rr)
    ld_lrow = load(8, lrow_h, lrow)
    ld_k2 = load(4, k2_h, kk.at[0])
    ld_place = load(6, place_h, place)
    ld_k1 = load(5, k1_h, kk.at[1])
    ld_exp = load(13, exp_h, expm)

    @pl.when(d == 0)
    def _():
        g2x[0:2] = jnp.zeros((2, NW, RC), BF16)
        pfx[0:1] = jnp.zeros((1, NW, RC), BF16)
        hc[96:128] = jnp.zeros((32, RC), BF16)

    @pl.when(d == ND - 1)
    def _():
        g2x[18:20] = jnp.zeros((2, NW, RC), BF16)
        pfx[17:18] = jnp.zeros((1, NW, RC), BF16)
        hc[128:160] = jnp.zeros((32, RC), BF16)

    def build_mixers():
        ld_k2.wait()
        ld_k1.wait()
        ld_place.wait()
        eye = (
            lax.broadcasted_iota(jnp.int32, (C, C), 0) == lax.broadcasted_iota(jnp.int32, (C, C), 1)
        ).astype(BF16)
        for layer, w in enumerate((w2, w1)):
            for pair in range(9):
                kc[layer, pl.ds(pair * C, C)] = lax.dot_general(
                    eye, kk[layer, pair], (((1,), (1,)), ((), ())), preferred_element_type=F32
                ).astype(BF16)
            for r_in in range(ROWS):
                mixed = jnp.dot(kc[layer], place[layer, r_in], preferred_element_type=F32)
                w[:, pl.ds(r_in * C, C), :] = mixed.astype(BF16).reshape(9, C, RC)

    def build_resample():
        ld_rr.wait()
        ld_lrow.wait()
        eye16 = (
            lax.broadcasted_iota(jnp.int32, (NS, NS), 0) == lax.broadcasted_iota(jnp.int32, (NS, NS), 1)
        ).astype(BF16)
        own_row = (
            lax.broadcasted_iota(jnp.int32, (ROWS * NS, ROWS * ROWS), 0) // NS
            == lax.broadcasted_iota(jnp.int32, (ROWS * NS, ROWS * ROWS), 1) // ROWS
        )
        for k in range(CAMS):
            turned = lax.dot_general(
                eye16, rr[k].astype(BF16), (((1,), (1,)), ((), ())), preferred_element_type=F32
            )
            picked = jnp.where(own_row, jnp.concatenate([turned] * ROWS, axis=0), 0.0)
            lbuf[pl.ds(k * NS * ROWS, NS * ROWS)] = jnp.dot(
                picked.astype(BF16), lrow[k], preferred_element_type=F32
            )
        chan_row = lax.broadcasted_iota(jnp.int32, (16, 128), 0)
        chan_lane = lax.rem(lax.broadcasted_iota(jnp.int32, (16, 128), 1), 16)
        chan_same = (chan_row == chan_lane).astype(F32)

        def build_rt(s, carry):
            for k in range(CAMS):
                for r in range(ROWS):
                    row = lbuf[pl.ds((k * ROWS + r) * NS + s, 1)]
                    rt[s, r * 16 : (r + 1) * 16, k * 128 : (k + 1) * 128] = (
                        jnp.broadcast_to(row, (16, 128)) * chan_same
                    ).astype(BF16)
            return carry

        lax.fori_loop(0, NS, build_rt, 0)

    def build_bands():
        ld_taps.wait()
        ld_width.wait()
        ld_off.wait()
        ld_slane.wait()
        lanes = NS * NW
        width_l = jnp.dot(width[...].astype(F32).astype(BF16), slane[...], preferred_element_type=F32)
        off_l = jnp.dot(off[...].astype(F32).astype(BF16), slane[...], preferred_element_type=F32)
        tap_index = lax.broadcasted_iota(jnp.int32, (TAPS, lanes), 0).astype(F32)
        u_lane = lax.rem(lax.broadcasted_iota(jnp.int32, (1, lanes), 1), NW).astype(F32)
        w_row = lax.broadcasted_iota(jnp.int32, (16, lanes), 0).astype(F32).astype(BF16)
        for k in range(CAMS):
            taps_l = jnp.dot(taps[k].astype(BF16), slane[...], preferred_element_type=F32)
            taps_l = jnp.where(tap_index < width_l[k : k + 1], taps_l, 0.0)
            wide = [
                jnp.broadcast_to(taps_l[j : j + 1], (16, lanes)).astype(BF16) for j in range(TAPS)
            ]
            start = jnp.broadcast_to(u_lane + 32.0 - off_l[k : k + 1], (16, lanes)).astype(BF16) - w_row

            def build_band(block, carry):
                gap = start - lax.rem(block * 16 + 96, 128).astype(F32).astype(BF16)
                value = jnp.zeros((16, lanes), BF16)
                for j in range(TAPS):
                    value = jnp.where(gap == jnp.asarray(j, BF16), wide[j], value)
                band[k, pl.ds(pl.multiple_of(block * 16, 16), 16)] = value
                return carry

            lax.fori_loop(0, 8, build_band, 0)

    if EARLYB:
        build_bands()
    if EARLYR:
        build_resample()
    if EARLYW:
        build_mixers()
    ld_cot.wait()
    ld_pre2.wait()
    g2x[2:18] = jnp.where(pre2[...] > 0, cot[...], jnp.zeros((), BF16))
    ld_pre1.wait()
    ld_sel.wait()
    acc = jnp.zeros((160, RC), F32)
    for part, ref in enumerate((g2x.at[2:18, 0:16], g2x.at[2:18, 48:64],
                                pfx.at[1:17, 0:16], pfx.at[1:17, 48:64])):
        acc = acc + jnp.dot(
            sel[:, 256 * part : 256 * part + 256], ref[...].reshape(256, RC),
            preferred_element_type=F32,
        )
    stage[...] = acc.astype(BF16)

    pl.semaphore_wait(barrier, 3 * ND - 1)

    def remote(group, src, dst, dep, col):
        return pltpu.make_async_remote_copy(
            src_ref=src, dst_ref=dst, send_sem=fs_sem.at[group], recv_sem=fr_sem.at[group],
            device_id={"depth": dep, "azim": col}, device_id_type=pl.DeviceIdType.MESH,
        )

    up = jnp.minimum(d + 1, ND - 1)
    dn = jnp.maximum(d - 1, 0)
    to_up = [
        remote(1, g2x.at[pl.ds(16, 2)], g2x.at[pl.ds(0, 2)], up, a),
        remote(1, pfx.at[pl.ds(16, 1)], pfx.at[pl.ds(0, 1)], up, a),
        remote(1, stage.at[pl.ds(96, 16)], hc.at[pl.ds(96, 16)], up, a_up),
        remote(1, stage.at[pl.ds(112, 16)], hc.at[pl.ds(112, 16)], up, a_dn),
    ]
    to_dn = [
        remote(2, g2x.at[pl.ds(2, 2)], g2x.at[pl.ds(18, 2)], dn, a),
        remote(2, pfx.at[pl.ds(1, 1)], pfx.at[pl.ds(17, 1)], dn, a),
        remote(2, stage.at[pl.ds(128, 16)], hc.at[pl.ds(128, 16)], dn, a_up),
        remote(2, stage.at[pl.ds(144, 16)], hc.at[pl.ds(144, 16)], dn, a_dn),
    ]
    sides = [
        remote(0, stage.at[pl.ds(0, 48)], hc.at[pl.ds(0, 48)], d, a_up),
        remote(0, stage.at[pl.ds(48, 48)], hc.at[pl.ds(48, 48)], d, a_dn),
    ]
    for copy in sides:
        copy.start()

    @pl.when(d < ND - 1)
    def _():
        for copy in to_up:
            copy.start()

    @pl.when(d > 0)
    def _():
        for copy in to_dn:
            copy.start()

    def drain(sem, rows):
        view = w2.at[0, pl.ds(0, rows)]
        pltpu.make_async_copy(view, view, sem).wait()

    if not EARLYW:
        build_mixers()
    if not EARLYR:
        build_resample()
    if not EARLYB:
        build_bands()

    row16 = lax.broadcasted_iota(jnp.int32, (16, RC), 0)
    is0, is1, is14, is15 = (row16 == n for n in (0, 1, 14, 15))
    row64 = lax.broadcasted_iota(jnp.int32, (NW, RC), 0)

    def build_s1(e, carry):
        x = g2x[e].astype(F32)
        ahead = pltpu.roll(x, NW - 1, 0)
        behind = pltpu.roll(x, 1, 0)
        s1[e, :, 0:RC] = jnp.where(row64 == NW - 1, 0.0, ahead).astype(BF16)
        s1[e, :, RC : 2 * RC] = g2x[e]
        s1[e, :, 2 * RC :] = jnp.where(row64 == 0, 0.0, behind).astype(BF16)
        t1[e, :, 0:RC] = jnp.where(is1, behind[0:16], 0.0).astype(BF16)
        t1[e, :, 2 * RC :] = jnp.where(is14, ahead[48:64], 0.0).astype(BF16)
        return carry

    def joined(rows, w):
        total = 0.0
        for td in range(3):
            total = total + jnp.dot(
                rows[td], w[3 * td : 3 * td + 3].reshape(3 * RC, RC), preferred_element_type=F32
            )
        return total

    def gated(f, h):
        x = jnp.where(pfx[f].astype(F32) > 0, h, 0.0)
        s2[f, :, 0:RC] = pltpu.roll(x, NW - 1, 0).astype(BF16)
        s2[f, :, RC : 2 * RC] = x.astype(BF16)
        s2[f, :, 2 * RC :] = pltpu.roll(x, 1, 0).astype(BF16)

    def conv1(chunk, carry):
        base = 2 + chunk * CH1
        rows = [s1[pl.ds(base + 2 - td, CH1)].reshape(CH1 * NW, 3 * RC) for td in range(3)]
        total = joined(rows, w2).reshape(CH1, NW, RC)
        for n in range(CH1):
            hidden[base + n, 0:16] = total[n, 0:16]
            hidden[base + n, 16:32] = total[n, 48:64]
            gated(base + n, total[n])
        return carry

    lax.fori_loop(2, 18, build_s1, 0, unroll=2)
    lax.fori_loop(0, 14 // CH1, conv1, 0)

    ld_exp.wait()
    drain(fr_sem.at[0], 96)

    @pl.when(d < ND - 1)
    def _():
        drain(fr_sem.at[2], 224)

    @pl.when(d > 0)
    def _():
        drain(fr_sem.at[1], 224)

    edges[...] = jnp.dot(expm[...], hc[...], preferred_element_type=F32)
    for e in (0, 1, 18, 19):
        build_s1(e, 0)

    def add_edges(e, carry):
        tile = [edges[pl.ds(pl.multiple_of((20 * n + e) * 16, 16), 16)].astype(BF16) for n in range(3)]
        t1[e, :, 0:RC] = t1[e, :, 0:RC] + tile[0]
        t1[e, :, RC : 2 * RC] = tile[1]
        t1[e, :, 2 * RC :] = t1[e, :, 2 * RC :] + tile[2]
        return carry

    lax.fori_loop(0, 20, add_edges, 0, unroll=4)
    fix[...] = joined(
        [t1[2 - td : 20 - td].reshape(18 * 16, 3 * RC) for td in range(3)], w2
    ).reshape(18, 16, RC)
    for f in (0, 16):
        total = joined(
            [s1[f + 2 - td : f + 4 - td].reshape(2 * NW, 3 * RC) for td in range(3)], w2
        ).reshape(2, NW, RC)
        for n in range(2):
            hidden[f + n, 0:16] = total[n, 0:16]
            hidden[f + n, 16:32] = total[n, 48:64]
            gated(f + n, total[n])

    def build_s2(f, carry):
        c = fix[f]
        left = jnp.where(is0, hidden[f, 0:16] + c, hidden[f, 0:16])
        right = jnp.where(is15, hidden[f, 16:32] + c, hidden[f, 16:32])
        left = jnp.where(pfx[f, 0:16].astype(F32) > 0, left, 0.0)
        right = jnp.where(pfx[f, 48:64].astype(F32) > 0, right, 0.0)
        gate = edges[pl.ds(pl.multiple_of((60 + f) * 16, 16), 16)]
        side = jnp.where(gate > 0, c, 0.0)
        s2[f, 0:16, RC : 2 * RC] = left.astype(BF16)
        s2[f, 48:64, RC : 2 * RC] = right.astype(BF16)
        s2[f, 48:64, 0:RC] = jnp.where(is15, pltpu.roll(side, 1, 0), pltpu.roll(right, 15, 0)).astype(BF16)
        s2[f, 0:16, 2 * RC :] = jnp.where(is0, pltpu.roll(side, 15, 0), pltpu.roll(left, 1, 0)).astype(BF16)
        return carry

    lax.fori_loop(0, 18, build_s2, 0, unroll=US2)

    def conv2(chunk, carry):
        base = chunk * CH2
        rows = [s2[pl.ds(base + 2 - td, CH2)].reshape(CH2 * NW, 3 * RC) for td in range(3)]
        total = joined(rows, w1)
        vol[pl.ds(base, CH2)] = total.astype(BF16).reshape(CH2, NW, RC)
        return carry

    lax.fori_loop(0, NS // CH2, conv2, 0, unroll=True)

    def mix(s, carry):
        v = jnp.concatenate([vol[s, :, 0:128], vol[s, :, 128:256]], axis=0)
        y = jnp.dot(v, rt[s], preferred_element_type=F32).astype(BF16)
        for k in range(CAMS):
            ymix[k, s, :, 0:128] = y[0:64, k * 128 : k * 128 + 128]
            ymix[k, s, :, 128:256] = y[64:128, k * 128 : k * 128 + 128]
        return carry

    lax.fori_loop(0, NS, mix, 0, unroll=True)

    block = lax.broadcasted_iota(jnp.int32, (1, 16, 128), 2) // 16

    def back(j, src_row, rows, dst_row, col):
        pltpu.make_async_remote_copy(
            src_ref=zbuf.at[j, pl.ds(src_row, rows)],
            dst_ref=rbuf.at[pl.ds(j * 128 + dst_row, rows)],
            send_sem=bs_sem, recv_sem=br_sem,
            device_id={"depth": lax.rem(d + j, ND), "azim": col},
            device_id_type=pl.DeviceIdType.MESH,
        ).start()

    order = list(range(1, ND)) + [0]
    slots = [
        lax.rem(block - lax.rem(d + j, ND) + ND, ND).astype(F32).astype(BF16) for j in range(ND)
    ]
    for part in range(2):
        source = []
        for k in range(CAMS):
            cam = jnp.dot(
                band[k, part * 64 : part * 64 + 64], ymix[k].reshape(NS * NW, RC),
                preferred_element_type=F32,
            )
            source.append(cam[:, 0:128].astype(BF16).reshape(4, 16, 128))
            source.append(pltpu.roll(cam[:, 128:256], 16, 1).astype(BF16).reshape(4, 16, 128))
        for j in order:
            z = source[0]
            for q in range(1, ROWS):
                z = jnp.where(slots[j] == jnp.asarray(q, BF16), source[q], z)
            if part == 1 and j == 0:
                rbuf[0:64] = z.reshape(64, 128)
                continue
            zbuf[j, part * 64 : part * 64 + 64] = z.reshape(64, 128)
            if part == 0:
                back(j, 0, 32, 64, a_up)
                back(j, 32, 32, 96, a_dn)
            else:
                back(j, 64, 64, 0, a)

    arrived = rbuf.at[pl.ds(64, ND * 128 - 64)]
    pltpu.make_async_copy(arrived, arrived, br_sem).wait()
    total = jnp.zeros((NW, 128), F32)
    for j in range(ND):
        own = rbuf[j * 128 : j * 128 + 64].astype(F32)
        total = total + (own + rbuf[j * 128 + 64 : j * 128 + 128].astype(F32))
    out_ref[0] = pltpu.roll(total, lax.rem(ND - d, ND) * 16, 1)

    pltpu.make_async_copy(arrived, arrived, bs_sem).wait()
    drain(fs_sem.at[0], 96)

    @pl.when(d < ND - 1)
    def _():
        drain(fs_sem.at[1], 224)

    @pl.when(d > 0)
    def _():
        drain(fs_sem.at[2], 224)


def body(cotangent, pre_second, pre_first, kernel_first, kernel_second, row_resample, col_taps, band_width, col_offset):
    consts = [
        jnp.asarray(x, BF16)
        for x in (stage_select(), edge_expand(), row_place(), lane_rows(), sphere_lanes())
    ]
    vm = pltpu.VMEM
    scratch = [
        vm((NS, NW, RC), BF16), vm((NS, NW, RC), BF16), vm((18, NW, RC), BF16),
        vm((20, NW, RC), BF16), vm((2, 9, 96, C), BF16), vm((CAMS, ROWS * ROWS, NS), F32),
        vm((CAMS, TAPS, NS), F32), vm((CAMS, NS), jnp.int32), vm((CAMS, NS), jnp.int32),
        vm((160, 1024), BF16), vm((78 * 16, 160), BF16), vm((2, ROWS, 96, RC), BF16),
        vm((CAMS, ROWS * ROWS, 128), BF16), vm((NS, NS * NW), BF16),
        vm((160, RC), BF16), vm((160, RC), BF16),
        vm((20, NW, 3 * RC), BF16), vm((20, 16, 3 * RC), BF16), vm((18, NW, 3 * RC), BF16),
        vm((18, 32, RC), F32), vm((18, 16, RC), F32), vm((78 * 16, RC), F32), vm((2, 288, 96), BF16),
        vm((9, RC, RC), BF16), vm((9, RC, RC), BF16),
        vm((CAMS * NS * ROWS, 128), F32), vm((NS, 128, CAMS * 128), BF16),
        vm((CAMS, 128, NS * NW), BF16), vm((NS, NW, RC), BF16), vm((CAMS, NS, NW, RC), BF16),
        vm((ROWS, 128, 128), BF16), vm((ND * 128, 128), BF16),
        pltpu.SemaphoreType.DMA((14,)), pltpu.SemaphoreType.DMA((3,)),
        pltpu.SemaphoreType.DMA((3,)), pltpu.SemaphoreType.DMA, pltpu.SemaphoreType.DMA,
    ]
    return pl.pallas_call(
        kernel,
        out_shape=jax.ShapeDtypeStruct((1, NW, 128), F32),
        in_specs=[pl.BlockSpec(memory_space=pl.ANY)] * 14,
        out_specs=pl.BlockSpec(memory_space=pltpu.VMEM),
        scratch_shapes=scratch,
        compiler_params=pltpu.CompilerParams(
            collective_id=0, has_side_effects=True, vmem_limit_bytes=62 * 1024 * 1024
        ),
    )(
        cotangent, pre_second, pre_first,
        kernel_first.reshape(9, 96, C), kernel_second.reshape(9, 96, C),
        row_resample.transpose(0, 2, 3, 1).reshape(CAMS, ROWS * ROWS, NS), col_taps.transpose(0, 2, 1),
        band_width, col_offset, *consts,
    )


def solution(mesh):
    placed = (
        P("depth", "azim", None),
        P("depth", "azim", None),
        P("depth", "azim", None),
        P(),
        P(),
        P(None, "depth", None, None),
        P(None, "depth", None),
        P(None, "depth"),
        P(None, "depth"),
    )
    return jax.shard_map(
        body, mesh=mesh, in_specs=placed, out_specs=P("depth", "azim", None), check_vma=False
    )
```

```python
import numpy as np
import jax
import jax.numpy as jnp
from jax import lax
from jax.experimental import pallas as pl
from jax.experimental.pallas import tpu as pltpu
from jax.sharding import PartitionSpec as P

TAPS = 8
SHIFT = 24
NS = 16
NW = 64
ROWS = 8
C = 32
RC = ROWS * C
CAMS = 4
ND = 8
F32 = jnp.float32
BF16 = jnp.bfloat16
PARTS = 1
US2 = 3
CH1 = 7
CH2 = 8


def stage_select():
    sel = np.zeros((160, 1024), np.float32)

    def at(array, sphere, column):
        part = 2 * array + (0 if column < 16 else 1)
        return 256 * part + 16 * sphere + column % 16

    for s in range(NS):
        sel[s, at(0, s, 62)] = 1
        sel[16 + s, at(0, s, 63)] = 1
        sel[32 + s, at(1, s, 63)] = 1
        sel[48 + s, at(0, s, 0)] = 1
        sel[64 + s, at(0, s, 1)] = 1
        sel[80 + s, at(1, s, 0)] = 1
    corners = ((96, 14, 62), (112, 14, 0), (128, 0, 62), (144, 0, 0))
    for base, sphere, column in corners:
        for i in range(4):
            sel[base + i, at(0, sphere + i // 2, column + i % 2)] = 1
        pf_sphere = 15 if sphere == 14 else 0
        pf_column = 63 if column == 62 else 0
        sel[base + 4, at(1, pf_sphere, pf_column)] = 1
    return sel


def edge_expand():
    mat = np.zeros((3 * 20 + 18, 16, 160), np.float32)
    for e in range(20):
        if e < 2:
            left, right = [96 + 2 * e, 97 + 2 * e], [112 + 2 * e, 113 + 2 * e]
        elif e < 18:
            left, right = [e - 2, 16 + e - 2], [48 + e - 2, 64 + e - 2]
        else:
            f = e - 18
            left, right = [128 + 2 * f, 129 + 2 * f], [144 + 2 * f, 145 + 2 * f]
        mat[e, 14, right[1]] = 1
        mat[e, 15, right[0]] = 1
        mat[20 + e, 1, left[1]] = 1
        mat[20 + e, 14, right[0]] = 1
        mat[40 + e, 0, left[1]] = 1
        mat[40 + e, 1, left[0]] = 1
    for f in range(18):
        left = 100 if f == 0 else 132 if f == 17 else 32 + f - 1
        right = 116 if f == 0 else 148 if f == 17 else 80 + f - 1
        mat[60 + f, 1, left] = 1
        mat[60 + f, 14, right] = 1
    return mat.reshape(-1, 160)


def row_place():
    place = np.zeros((2, ROWS, 3, C, RC), np.float32)
    i = np.arange(C)
    for r_in in range(ROWS):
        for tap in range(3):
            r_out = r_in - 1 + tap
            if 0 <= r_out < ROWS:
                place[0, r_in, tap, i, r_out * C + i] = 1
                place[1, r_in, tap, i, (i // 16) * 128 + r_out * 16 + i % 16] = 1
    return place.reshape(2, ROWS, 3 * C, RC)


def lane_rows():
    out = np.zeros((CAMS, ROWS, ROWS, 128), np.float32)
    lane = np.arange(128)
    for k in range(CAMS):
        out[k, :, (lane // 16 - 2 * k) % 8, lane] = 1
    return out.reshape(CAMS, ROWS * ROWS, 128)


def kernel(
    cot_h, pre2_h, pre1_h, k1_h, k2_h, rr_h, taps_h, width_h, off_h,
    sel_h, exp_h, place_h, lrow_h,
    out_ref,
    cot, pre2, pfx, g2x, kk, rr, taps, width, off,
    sel, expm, place, lrow, base,
    stage, hc, s1, t1, s2, hidden, fix, edges, kc, w2, w1, lbuf, rt, band, vol, ymix, zbuf, rbuf,
    in_sem, fs_sem, fr_sem, bs_sem, br_sem,
):
    d = lax.axis_index("depth")
    a = lax.axis_index("azim")
    na = lax.axis_size("azim")
    a_up = lax.rem(a + 1, na)
    a_dn = lax.rem(a + na - 1, na)

    def load(i, src, dst):
        copy = pltpu.make_async_copy(src, dst, in_sem.at[i])
        copy.start()
        return copy

    ld_parts = []
    for part in range(PARTS):
        span = pl.ds(part * (NS // PARTS), NS // PARTS)
        ld_parts.append(load(13 + 2 * part, cot_h.at[span], cot.at[span]))
        ld_parts.append(load(14 + 2 * part, pre2_h.at[span], pre2.at[span]))
    ld_taps = load(9, taps_h, taps)
    ld_width = load(10, width_h, width)
    ld_off = load(11, off_h, off)

    barrier = pltpu.get_barrier_semaphore()
    for j in range(ND):
        t = lax.rem(d + j, ND)
        for col in (a_dn, a, a_up):
            if j == 0 and col is a:
                continue
            pl.semaphore_signal(
                barrier, inc=1, device_id={"depth": t, "azim": col},
                device_id_type=pl.DeviceIdType.MESH,
            )

    ld_pre1 = load(2, pre1_h, pfx.at[pl.ds(1, NS)])
    ld_sel = load(3, sel_h, sel)
    ld_rr = load(7, rr_h, rr)
    ld_lrow = load(8, lrow_h, lrow)
    ld_k2 = load(4, k2_h, kk.at[0])
    ld_place = load(6, place_h, place)
    ld_k1 = load(5, k1_h, kk.at[1])
    ld_exp = load(1, exp_h, expm)

    @pl.when(d == 0)
    def _():
        g2x[0:2] = jnp.zeros((2, NW, RC), BF16)
        pfx[0:1] = jnp.zeros((1, NW, RC), BF16)
        hc[96:128] = jnp.zeros((32, RC), BF16)

    @pl.when(d == ND - 1)
    def _():
        g2x[18:20] = jnp.zeros((2, NW, RC), BF16)
        pfx[17:18] = jnp.zeros((1, NW, RC), BF16)
        hc[128:160] = jnp.zeros((32, RC), BF16)

    eye16 = (
        lax.broadcasted_iota(jnp.int32, (NS, NS), 0) == lax.broadcasted_iota(jnp.int32, (NS, NS), 1)
    ).astype(BF16)

    def build_mixers():
        ld_k2.wait()
        ld_k1.wait()
        ld_place.wait()
        eye = (
            lax.broadcasted_iota(jnp.int32, (C, C), 0) == lax.broadcasted_iota(jnp.int32, (C, C), 1)
        ).astype(BF16)
        for layer, w in enumerate((w2, w1)):
            for pair in range(9):
                kc[layer, pl.ds(pair * C, C)] = lax.dot_general(
                    eye, kk[layer, pair], (((1,), (1,)), ((), ())), preferred_element_type=F32
                ).astype(BF16)
            for r_in in range(ROWS):
                mixed = jnp.dot(kc[layer], place[layer, r_in], preferred_element_type=F32)
                w[:, pl.ds(r_in * C, C), :] = mixed.astype(BF16).reshape(9, C, RC)

    def build_resample():
        ld_rr.wait()
        ld_lrow.wait()
        own_row = (
            lax.broadcasted_iota(jnp.int32, (ROWS * NS, ROWS * ROWS), 0) // NS
            == lax.broadcasted_iota(jnp.int32, (ROWS * NS, ROWS * ROWS), 1) // ROWS
        )
        for k in range(CAMS):
            turned = lax.dot_general(
                eye16, rr[k].astype(BF16), (((1,), (1,)), ((), ())), preferred_element_type=F32
            )
            picked = jnp.where(own_row, jnp.concatenate([turned] * ROWS, axis=0), 0.0)
            lbuf[pl.ds(k * NS * ROWS, NS * ROWS)] = jnp.dot(
                picked.astype(BF16), lrow[k], preferred_element_type=F32
            )
        chan_row = lax.broadcasted_iota(jnp.int32, (16, 128), 0)
        chan_lane = lax.rem(lax.broadcasted_iota(jnp.int32, (16, 128), 1), 16)
        chan_same = (chan_row == chan_lane).astype(F32)

        def build_rt(s, carry):
            for k in range(CAMS):
                for r in range(ROWS):
                    row = lbuf[pl.ds((k * ROWS + r) * NS + s, 1)]
                    rt[s, r * 16 : (r + 1) * 16, k * 128 : (k + 1) * 128] = (
                        jnp.broadcast_to(row, (16, 128)) * chan_same
                    ).astype(BF16)
            return carry

        lax.fori_loop(0, NS, build_rt, 0)

    def build_bands():
        ld_taps.wait()
        ld_width.wait()
        ld_off.wait()
        def turned(x):
            return lax.dot_general(
                eye16, x.astype(F32).astype(BF16), (((1,), (1,)), ((), ())),
                preferred_element_type=F32,
            )

        offs, widths = turned(off[...]), turned(width[...])
        lane = lax.broadcasted_iota(jnp.int32, (NS, 128), 1)
        odd = lax.rem(lax.broadcasted_iota(jnp.int32, (NS, 128), 0), 2)
        place_lane = lax.rem(lane - 64 * odd + 128, 128).astype(F32)
        low = lax.broadcasted_iota(jnp.int32, (128, 128), 1) < 64
        for k in range(CAMS):
            tap = turned(taps[k])
            start = offs[:, k : k + 1] - 32.0
            start = jnp.where(start < 0, start + 128.0, start)
            gap = place_lane - start
            gap = jnp.where(gap < 0, gap + 128.0, gap)
            value = jnp.zeros((NS, 128), F32)
            for j in range(TAPS):
                keep = (gap == float(j)) & (widths[:, k : k + 1] > float(j))
                value = jnp.where(keep, tap[:, j : j + 1], value)
            base[k] = value
        def roll_bands(pair, carry):
            for k in range(CAMS):
                two = [
                    pltpu.roll(
                        jnp.broadcast_to(base[k, pl.ds(2 * pair + n, 1)], (128, 128)),
                        96, 1, stride=1, stride_axis=0,
                    )
                    for n in range(2)
                ]
                band[k, :, pl.ds(pl.multiple_of(pair * 128, 128), 128)] = jnp.where(
                    low, two[0], two[1]
                ).astype(BF16)
            return carry

        lax.fori_loop(0, NS // 2, roll_bands, 0)

    build_bands()
    for part in range(PARTS):
        ld_parts[2 * part].wait()
        ld_parts[2 * part + 1].wait()
        span = pl.ds(part * (NS // PARTS), NS // PARTS)
        g2x[pl.ds(2 + part * (NS // PARTS), NS // PARTS)] = jnp.where(
            pre2[span] > 0, cot[span], jnp.zeros((), BF16)
        )
    ld_pre1.wait()
    ld_sel.wait()
    acc = jnp.zeros((160, RC), F32)
    for part, ref in enumerate((g2x.at[2:18, 0:16], g2x.at[2:18, 48:64],
                                pfx.at[1:17, 0:16], pfx.at[1:17, 48:64])):
        acc = acc + jnp.dot(
            sel[:, 256 * part : 256 * part + 256], ref[...].reshape(256, RC),
            preferred_element_type=F32,
        )
    stage[...] = acc.astype(BF16)

    pl.semaphore_wait(barrier, 3 * ND - 1)

    def remote(group, src, dst, dep, col):
        return pltpu.make_async_remote_copy(
            src_ref=src, dst_ref=dst, send_sem=fs_sem.at[group], recv_sem=fr_sem.at[group],
            device_id={"depth": dep, "azim": col}, device_id_type=pl.DeviceIdType.MESH,
        )

    up = jnp.minimum(d + 1, ND - 1)
    dn = jnp.maximum(d - 1, 0)
    to_up = [
        remote(1, g2x.at[pl.ds(16, 2)], g2x.at[pl.ds(0, 2)], up, a),
        remote(1, pfx.at[pl.ds(16, 1)], pfx.at[pl.ds(0, 1)], up, a),
        remote(1, stage.at[pl.ds(96, 16)], hc.at[pl.ds(96, 16)], up, a_up),
        remote(1, stage.at[pl.ds(112, 16)], hc.at[pl.ds(112, 16)], up, a_dn),
    ]
    to_dn = [
        remote(2, g2x.at[pl.ds(2, 2)], g2x.at[pl.ds(18, 2)], dn, a),
        remote(2, pfx.at[pl.ds(1, 1)], pfx.at[pl.ds(17, 1)], dn, a),
        remote(2, stage.at[pl.ds(128, 16)], hc.at[pl.ds(128, 16)], dn, a_up),
        remote(2, stage.at[pl.ds(144, 16)], hc.at[pl.ds(144, 16)], dn, a_dn),
    ]
    sides = [
        remote(0, stage.at[pl.ds(0, 48)], hc.at[pl.ds(0, 48)], d, a_up),
        remote(0, stage.at[pl.ds(48, 48)], hc.at[pl.ds(48, 48)], d, a_dn),
    ]
    for copy in sides:
        copy.start()

    @pl.when(d < ND - 1)
    def _():
        for copy in to_up:
            copy.start()

    @pl.when(d > 0)
    def _():
        for copy in to_dn:
            copy.start()

    def drain(sem, rows):
        view = w2.at[0, pl.ds(0, rows)]
        pltpu.make_async_copy(view, view, sem).wait()

    build_mixers()
    build_resample()

    row16 = lax.broadcasted_iota(jnp.int32, (16, RC), 0)
    is0, is1, is14, is15 = (row16 == n for n in (0, 1, 14, 15))
    row64 = lax.broadcasted_iota(jnp.int32, (NW, RC), 0)

    def build_s1(e, carry):
        x = g2x[e].astype(F32)
        ahead = pltpu.roll(x, NW - 1, 0)
        behind = pltpu.roll(x, 1, 0)
        s1[e, :, 0:RC] = jnp.where(row64 == NW - 1, 0.0, ahead).astype(BF16)
        s1[e, :, RC : 2 * RC] = g2x[e]
        s1[e, :, 2 * RC :] = jnp.where(row64 == 0, 0.0, behind).astype(BF16)
        t1[e, :, 0:RC] = jnp.where(is1, behind[0:16], 0.0).astype(BF16)
        t1[e, :, 2 * RC :] = jnp.where(is14, ahead[48:64], 0.0).astype(BF16)
        return carry

    def joined(rows, w):
        total = 0.0
        for td in range(3):
            total = total + jnp.dot(
                rows[td], w[3 * td : 3 * td + 3].reshape(3 * RC, RC), preferred_element_type=F32
            )
        return total

    def gated(f, h):
        x = jnp.where(pfx[f].astype(F32) > 0, h, 0.0)
        s2[f, :, 0:RC] = pltpu.roll(x, NW - 1, 0).astype(BF16)
        s2[f, :, RC : 2 * RC] = x.astype(BF16)
        s2[f, :, 2 * RC :] = pltpu.roll(x, 1, 0).astype(BF16)

    def conv1(chunk, carry):
        base = 2 + chunk * CH1
        rows = [s1[pl.ds(base + 2 - td, CH1)].reshape(CH1 * NW, 3 * RC) for td in range(3)]
        total = joined(rows, w2).reshape(CH1, NW, RC)
        for n in range(CH1):
            hidden[base + n, 0:16] = total[n, 0:16]
            hidden[base + n, 16:32] = total[n, 48:64]
            gated(base + n, total[n])
        return carry

    lax.fori_loop(2, 18, build_s1, 0, unroll=2)
    lax.fori_loop(0, 14 // CH1, conv1, 0)

    ld_exp.wait()
    drain(fr_sem.at[0], 96)

    @pl.when(d < ND - 1)
    def _():
        drain(fr_sem.at[2], 224)

    @pl.when(d > 0)
    def _():
        drain(fr_sem.at[1], 224)

    edges[...] = jnp.dot(expm[...], hc[...], preferred_element_type=F32)
    for e in (0, 1, 18, 19):
        build_s1(e, 0)

    def add_edges(e, carry):
        tile = [edges[pl.ds(pl.multiple_of((20 * n + e) * 16, 16), 16)].astype(BF16) for n in range(3)]
        t1[e, :, 0:RC] = t1[e, :, 0:RC] + tile[0]
        t1[e, :, RC : 2 * RC] = tile[1]
        t1[e, :, 2 * RC :] = t1[e, :, 2 * RC :] + tile[2]
        return carry

    lax.fori_loop(0, 20, add_edges, 0, unroll=4)
    fix[...] = joined(
        [t1[2 - td : 20 - td].reshape(18 * 16, 3 * RC) for td in range(3)], w2
    ).reshape(18, 16, RC)
    for f in (0, 16):
        total = joined(
            [s1[f + 2 - td : f + 4 - td].reshape(2 * NW, 3 * RC) for td in range(3)], w2
        ).reshape(2, NW, RC)
        for n in range(2):
            hidden[f + n, 0:16] = total[n, 0:16]
            hidden[f + n, 16:32] = total[n, 48:64]
            gated(f + n, total[n])

    def build_s2(f, carry):
        c = fix[f]
        left = jnp.where(is0, hidden[f, 0:16] + c, hidden[f, 0:16])
        right = jnp.where(is15, hidden[f, 16:32] + c, hidden[f, 16:32])
        left = jnp.where(pfx[f, 0:16].astype(F32) > 0, left, 0.0)
        right = jnp.where(pfx[f, 48:64].astype(F32) > 0, right, 0.0)
        gate = edges[pl.ds(pl.multiple_of((60 + f) * 16, 16), 16)]
        side = jnp.where(gate > 0, c, 0.0)
        s2[f, 0:16, RC : 2 * RC] = left.astype(BF16)
        s2[f, 48:64, RC : 2 * RC] = right.astype(BF16)
        s2[f, 48:64, 0:RC] = jnp.where(is15, pltpu.roll(side, 1, 0), pltpu.roll(right, 15, 0)).astype(BF16)
        s2[f, 0:16, 2 * RC :] = jnp.where(is0, pltpu.roll(side, 15, 0), pltpu.roll(left, 1, 0)).astype(BF16)
        return carry

    lax.fori_loop(0, 18, build_s2, 0, unroll=US2)

    def conv2(chunk, carry):
        base = chunk * CH2
        rows = [s2[pl.ds(base + 2 - td, CH2)].reshape(CH2 * NW, 3 * RC) for td in range(3)]
        total = joined(rows, w1)
        vol[pl.ds(base, CH2)] = total.astype(BF16).reshape(CH2, NW, RC)
        return carry

    lax.fori_loop(0, NS // CH2, conv2, 0, unroll=True)

    def mix(s, carry):
        v = jnp.concatenate([vol[s, :, 0:128], vol[s, :, 128:256]], axis=0)
        y = jnp.dot(v, rt[s], preferred_element_type=F32).astype(BF16)
        for k in range(CAMS):
            ymix[k, s, :, 0:128] = y[0:64, k * 128 : k * 128 + 128]
            ymix[k, s, :, 128:256] = y[64:128, k * 128 : k * 128 + 128]
        return carry

    lax.fori_loop(0, NS, mix, 0, unroll=True)

    block = lax.broadcasted_iota(jnp.int32, (1, 16, 128), 2) // 16

    def back(j, src_row, rows, dst_row, col):
        pltpu.make_async_remote_copy(
            src_ref=zbuf.at[j, pl.ds(src_row, rows)],
            dst_ref=rbuf.at[pl.ds(j * 128 + dst_row, rows)],
            send_sem=bs_sem, recv_sem=br_sem,
            device_id={"depth": lax.rem(d + j, ND), "azim": col},
            device_id_type=pl.DeviceIdType.MESH,
        ).start()

    order = list(range(1, ND)) + [0]
    slots = [
        lax.rem(block - lax.rem(d + j, ND) + ND, ND).astype(F32).astype(BF16) for j in range(ND)
    ]
    for part in range(2):
        source = []
        for k in range(CAMS):
            cam = jnp.dot(
                band[k, part * 64 : part * 64 + 64], ymix[k].reshape(NS * NW, RC),
                preferred_element_type=F32,
            )
            source.append(cam[:, 0:128].astype(BF16).reshape(4, 16, 128))
            source.append(pltpu.roll(cam[:, 128:256], 16, 1).astype(BF16).reshape(4, 16, 128))
        for j in order:
            z = source[0]
            for q in range(1, ROWS):
                z = jnp.where(slots[j] == jnp.asarray(q, BF16), source[q], z)
            if part == 1 and j == 0:
                rbuf[0:64] = z.reshape(64, 128)
                continue
            zbuf[j, part * 64 : part * 64 + 64] = z.reshape(64, 128)
            if part == 0:
                back(j, 0, 32, 64, a_up)
                back(j, 32, 32, 96, a_dn)
            else:
                back(j, 64, 64, 0, a)

    arrived = rbuf.at[pl.ds(64, ND * 128 - 64)]
    pltpu.make_async_copy(arrived, arrived, br_sem).wait()
    total = jnp.zeros((NW, 128), F32)
    for j in range(ND):
        own = rbuf[j * 128 : j * 128 + 64].astype(F32)
        total = total + (own + rbuf[j * 128 + 64 : j * 128 + 128].astype(F32))
    out_ref[0] = pltpu.roll(total, lax.rem(ND - d, ND) * 16, 1)

    pltpu.make_async_copy(arrived, arrived, bs_sem).wait()
    drain(fs_sem.at[0], 96)

    @pl.when(d < ND - 1)
    def _():
        drain(fs_sem.at[1], 224)

    @pl.when(d > 0)
    def _():
        drain(fs_sem.at[2], 224)


def body(cotangent, pre_second, pre_first, kernel_first, kernel_second, row_resample, col_taps, band_width, col_offset):
    consts = [
        jnp.asarray(x, BF16)
        for x in (stage_select(), edge_expand(), row_place(), lane_rows())
    ]
    vm = pltpu.VMEM
    scratch = [
        vm((NS, NW, RC), BF16), vm((NS, NW, RC), BF16), vm((18, NW, RC), BF16),
        vm((20, NW, RC), BF16), vm((2, 9, 96, C), BF16), vm((CAMS, ROWS * ROWS, NS), F32),
        vm((CAMS, TAPS, NS), F32), vm((CAMS, NS), jnp.int32), vm((CAMS, NS), jnp.int32),
        vm((160, 1024), BF16), vm((78 * 16, 160), BF16), vm((2, ROWS, 96, RC), BF16),
        vm((CAMS, ROWS * ROWS, 128), BF16), vm((CAMS, NS, 128), F32),
        vm((160, RC), BF16), vm((160, RC), BF16),
        vm((20, NW, 3 * RC), BF16), vm((20, 16, 3 * RC), BF16), vm((18, NW, 3 * RC), BF16),
        vm((18, 32, RC), F32), vm((18, 16, RC), F32), vm((78 * 16, RC), F32), vm((2, 288, 96), BF16),
        vm((9, RC, RC), BF16), vm((9, RC, RC), BF16),
        vm((CAMS * NS * ROWS, 128), F32), vm((NS, 128, CAMS * 128), BF16),
        vm((CAMS, 128, NS * NW), BF16), vm((NS, NW, RC), BF16), vm((CAMS, NS, NW, RC), BF16),
        vm((ROWS, 128, 128), BF16), vm((ND * 128, 128), BF16),
        pltpu.SemaphoreType.DMA((13 + 2 * PARTS,)), pltpu.SemaphoreType.DMA((3,)),
        pltpu.SemaphoreType.DMA((3,)), pltpu.SemaphoreType.DMA, pltpu.SemaphoreType.DMA,
    ]
    return pl.pallas_call(
        kernel,
        out_shape=jax.ShapeDtypeStruct((1, NW, 128), F32),
        in_specs=[pl.BlockSpec(memory_space=pl.ANY)] * 13,
        out_specs=pl.BlockSpec(memory_space=pltpu.VMEM),
        scratch_shapes=scratch,
        compiler_params=pltpu.CompilerParams(
            collective_id=0, has_side_effects=True, vmem_limit_bytes=62 * 1024 * 1024
        ),
    )(
        cotangent, pre_second, pre_first,
        kernel_first.reshape(9, 96, C), kernel_second.reshape(9, 96, C),
        row_resample.transpose(0, 2, 3, 1).reshape(CAMS, ROWS * ROWS, NS), col_taps.transpose(0, 2, 1),
        band_width, col_offset, *consts,
    )


def solution(mesh):
    placed = (
        P("depth", "azim", None),
        P("depth", "azim", None),
        P("depth", "azim", None),
        P(),
        P(),
        P(None, "depth", None, None),
        P(None, "depth", None),
        P(None, "depth"),
        P(None, "depth"),
    )
    return jax.shard_map(
        body, mesh=mesh, in_specs=placed, out_specs=P("depth", "azim", None), check_vma=False
    )
```

```python
import numpy as np
import jax
import jax.numpy as jnp
from jax import lax
from jax.experimental import pallas as pl
from jax.experimental.pallas import tpu as pltpu
from jax.sharding import PartitionSpec as P

TAPS = 8
SHIFT = 24
NS = 16
NW = 64
ROWS = 8
C = 32
RC = ROWS * C
CAMS = 4
ND = 8
F32 = jnp.float32
BF16 = jnp.bfloat16
PARTS = 1
US2 = 3
CH1 = 7
CH2 = 8


def stage_select():
    sel = np.zeros((160, 1024), np.float32)

    def at(array, sphere, column):
        part = 2 * array + (0 if column < 16 else 1)
        return 256 * part + 16 * sphere + column % 16

    for s in range(NS):
        sel[s, at(0, s, 62)] = 1
        sel[16 + s, at(0, s, 63)] = 1
        sel[32 + s, at(1, s, 63)] = 1
        sel[48 + s, at(0, s, 0)] = 1
        sel[64 + s, at(0, s, 1)] = 1
        sel[80 + s, at(1, s, 0)] = 1
    corners = ((96, 14, 62), (112, 14, 0), (128, 0, 62), (144, 0, 0))
    for base, sphere, column in corners:
        for i in range(4):
            sel[base + i, at(0, sphere + i // 2, column + i % 2)] = 1
        pf_sphere = 15 if sphere == 14 else 0
        pf_column = 63 if column == 62 else 0
        sel[base + 4, at(1, pf_sphere, pf_column)] = 1
    return sel


def edge_expand():
    mat = np.zeros((3 * 20 + 18, 16, 160), np.float32)
    for e in range(20):
        if e < 2:
            left, right = [96 + 2 * e, 97 + 2 * e], [112 + 2 * e, 113 + 2 * e]
        elif e < 18:
            left, right = [e - 2, 16 + e - 2], [48 + e - 2, 64 + e - 2]
        else:
            f = e - 18
            left, right = [128 + 2 * f, 129 + 2 * f], [144 + 2 * f, 145 + 2 * f]
        mat[e, 14, right[1]] = 1
        mat[e, 15, right[0]] = 1
        mat[20 + e, 1, left[1]] = 1
        mat[20 + e, 14, right[0]] = 1
        mat[40 + e, 0, left[1]] = 1
        mat[40 + e, 1, left[0]] = 1
    for f in range(18):
        left = 100 if f == 0 else 132 if f == 17 else 32 + f - 1
        right = 116 if f == 0 else 148 if f == 17 else 80 + f - 1
        mat[60 + f, 1, left] = 1
        mat[60 + f, 14, right] = 1
    return mat.reshape(-1, 160)


def row_place():
    place = np.zeros((2, ROWS, 3, C, RC), np.float32)
    i = np.arange(C)
    for r_in in range(ROWS):
        for tap in range(3):
            r_out = r_in - 1 + tap
            if 0 <= r_out < ROWS:
                place[0, r_in, tap, i, r_out * C + i] = 1
                place[1, r_in, tap, i, (i // 16) * 128 + r_out * 16 + i % 16] = 1
    return place.reshape(2, ROWS, 3 * C, RC)


def lane_rows():
    out = np.zeros((CAMS, ROWS, ROWS, 128), np.float32)
    lane = np.arange(128)
    for k in range(CAMS):
        out[k, :, (lane // 16 - 2 * k) % 8, lane] = 1
    return out.reshape(CAMS, ROWS * ROWS, 128)


def kernel(
    cot_h, pre2_h, pre1_h, k1_h, k2_h, rr_h, taps_h, width_h, off_h,
    sel_h, exp_h, place_h, lrow_h,
    out_ref,
    cot, pre2, pfx, g2x, kk, rr, taps, width, off,
    sel, expm, place, lrow, base,
    stage, hc, s1, t1, s2, hidden, fix, edges, kc, w2, w1, lbuf, rt, band, vol, ymix, zbuf, rbuf,
    in_sem, fs_sem, fr_sem, bs_sem, br_sem,
):
    d = lax.axis_index("depth")
    a = lax.axis_index("azim")
    na = lax.axis_size("azim")
    a_up = lax.rem(a + 1, na)
    a_dn = lax.rem(a + na - 1, na)

    def load(i, src, dst):
        copy = pltpu.make_async_copy(src, dst, in_sem.at[i])
        copy.start()
        return copy

    ld_parts = []
    for part in range(PARTS):
        span = pl.ds(part * (NS // PARTS), NS // PARTS)
        ld_parts.append(load(13 + 2 * part, cot_h.at[span], cot.at[span]))
        ld_parts.append(load(14 + 2 * part, pre2_h.at[span], pre2.at[span]))
    ld_taps = load(9, taps_h, taps)
    ld_width = load(10, width_h, width)
    ld_off = load(11, off_h, off)

    barrier = pltpu.get_barrier_semaphore()
    for j in range(ND):
        t = lax.rem(d + j, ND)
        for col in (a_dn, a, a_up):
            if (j == 0 and col is a) or (1 < j < ND - 1 and col is not a):
                continue
            pl.semaphore_signal(
                barrier, inc=1, device_id={"depth": t, "azim": col},
                device_id_type=pl.DeviceIdType.MESH,
            )

    ld_pre1 = load(2, pre1_h, pfx.at[pl.ds(1, NS)])
    ld_sel = load(3, sel_h, sel)
    ld_rr = load(7, rr_h, rr)
    ld_lrow = load(8, lrow_h, lrow)
    ld_k2 = load(4, k2_h, kk.at[0])
    ld_place = load(6, place_h, place)
    ld_k1 = load(5, k1_h, kk.at[1])
    ld_exp = load(1, exp_h, expm)

    @pl.when(d == 0)
    def _():
        g2x[0:2] = jnp.zeros((2, NW, RC), BF16)
        pfx[0:1] = jnp.zeros((1, NW, RC), BF16)
        hc[96:128] = jnp.zeros((32, RC), BF16)

    @pl.when(d == ND - 1)
    def _():
        g2x[18:20] = jnp.zeros((2, NW, RC), BF16)
        pfx[17:18] = jnp.zeros((1, NW, RC), BF16)
        hc[128:160] = jnp.zeros((32, RC), BF16)

    eye16 = (
        lax.broadcasted_iota(jnp.int32, (NS, NS), 0) == lax.broadcasted_iota(jnp.int32, (NS, NS), 1)
    ).astype(BF16)

    def build_mixers():
        ld_k2.wait()
        ld_k1.wait()
        ld_place.wait()
        eye = (
            lax.broadcasted_iota(jnp.int32, (C, C), 0) == lax.broadcasted_iota(jnp.int32, (C, C), 1)
        ).astype(BF16)
        for layer, w in enumerate((w2, w1)):
            for pair in range(9):
                kc[layer, pl.ds(pair * C, C)] = lax.dot_general(
                    eye, kk[layer, pair], (((1,), (1,)), ((), ())), preferred_element_type=F32
                ).astype(BF16)
            for r_in in range(ROWS):
                mixed = jnp.dot(kc[layer], place[layer, r_in], preferred_element_type=F32)
                w[:, pl.ds(r_in * C, C), :] = mixed.astype(BF16).reshape(9, C, RC)

    def build_resample():
        ld_rr.wait()
        ld_lrow.wait()
        own_row = (
            lax.broadcasted_iota(jnp.int32, (ROWS * NS, ROWS * ROWS), 0) // NS
            == lax.broadcasted_iota(jnp.int32, (ROWS * NS, ROWS * ROWS), 1) // ROWS
        )
        for k in range(CAMS):
            turned = lax.dot_general(
                eye16, rr[k].astype(BF16), (((1,), (1,)), ((), ())), preferred_element_type=F32
            )
            picked = jnp.where(own_row, jnp.concatenate([turned] * ROWS, axis=0), 0.0)
            lbuf[pl.ds(k * NS * ROWS, NS * ROWS)] = jnp.dot(
                picked.astype(BF16), lrow[k], preferred_element_type=F32
            )
        chan_row = lax.broadcasted_iota(jnp.int32, (16, 128), 0)
        chan_lane = lax.rem(lax.broadcasted_iota(jnp.int32, (16, 128), 1), 16)
        chan_same = (chan_row == chan_lane).astype(F32)

        def build_rt(s, carry):
            for k in range(CAMS):
                for r in range(ROWS):
                    row = lbuf[pl.ds((k * ROWS + r) * NS + s, 1)]
                    rt[s, r * 16 : (r + 1) * 16, k * 128 : (k + 1) * 128] = (
                        jnp.broadcast_to(row, (16, 128)) * chan_same
                    ).astype(BF16)
            return carry

        lax.fori_loop(0, NS, build_rt, 0)

    def build_bands():
        ld_taps.wait()
        ld_width.wait()
        ld_off.wait()
        def turned(x):
            return lax.dot_general(
                eye16, x.astype(F32).astype(BF16), (((1,), (1,)), ((), ())),
                preferred_element_type=F32,
            )

        offs, widths = turned(off[...]), turned(width[...])
        lane = lax.broadcasted_iota(jnp.int32, (NS, 128), 1)
        odd = lax.rem(lax.broadcasted_iota(jnp.int32, (NS, 128), 0), 2)
        place_lane = lax.rem(lane - 64 * odd + 128, 128).astype(F32)
        low = lax.broadcasted_iota(jnp.int32, (128, 128), 1) < 64
        for k in range(CAMS):
            tap = turned(taps[k])
            start = offs[:, k : k + 1] - 32.0
            start = jnp.where(start < 0, start + 128.0, start)
            gap = place_lane - start
            gap = jnp.where(gap < 0, gap + 128.0, gap)
            value = jnp.zeros((NS, 128), F32)
            for j in range(TAPS):
                keep = (gap == float(j)) & (widths[:, k : k + 1] > float(j))
                value = jnp.where(keep, tap[:, j : j + 1], value)
            base[k] = value
        def roll_bands(pair, carry):
            for k in range(CAMS):
                two = [
                    pltpu.roll(
                        jnp.broadcast_to(base[k, pl.ds(2 * pair + n, 1)], (128, 128)),
                        96, 1, stride=1, stride_axis=0,
                    )
                    for n in range(2)
                ]
                band[k, :, pl.ds(pl.multiple_of(pair * 128, 128), 128)] = jnp.where(
                    low, two[0], two[1]
                ).astype(BF16)
            return carry

        lax.fori_loop(0, NS // 2, roll_bands, 0)

    build_bands()
    for part in range(PARTS):
        ld_parts[2 * part].wait()
        ld_parts[2 * part + 1].wait()
        span = pl.ds(part * (NS // PARTS), NS // PARTS)
        g2x[pl.ds(2 + part * (NS // PARTS), NS // PARTS)] = jnp.where(
            pre2[span] > 0, cot[span], jnp.zeros((), BF16)
        )
    ld_pre1.wait()
    ld_sel.wait()
    acc = jnp.zeros((160, RC), F32)
    for part, ref in enumerate((g2x.at[2:18, 0:16], g2x.at[2:18, 48:64],
                                pfx.at[1:17, 0:16], pfx.at[1:17, 48:64])):
        acc = acc + jnp.dot(
            sel[:, 256 * part : 256 * part + 256], ref[...].reshape(256, RC),
            preferred_element_type=F32,
        )
    stage[...] = acc.astype(BF16)

    pl.semaphore_wait(barrier, ND + 5)

    def remote(group, src, dst, dep, col):
        return pltpu.make_async_remote_copy(
            src_ref=src, dst_ref=dst, send_sem=fs_sem.at[group], recv_sem=fr_sem.at[group],
            device_id={"depth": dep, "azim": col}, device_id_type=pl.DeviceIdType.MESH,
        )

    up = jnp.minimum(d + 1, ND - 1)
    dn = jnp.maximum(d - 1, 0)
    to_up = [
        remote(1, g2x.at[pl.ds(16, 2)], g2x.at[pl.ds(0, 2)], up, a),
        remote(1, pfx.at[pl.ds(16, 1)], pfx.at[pl.ds(0, 1)], up, a),
        remote(1, stage.at[pl.ds(96, 16)], hc.at[pl.ds(96, 16)], up, a_up),
        remote(1, stage.at[pl.ds(112, 16)], hc.at[pl.ds(112, 16)], up, a_dn),
    ]
    to_dn = [
        remote(2, g2x.at[pl.ds(2, 2)], g2x.at[pl.ds(18, 2)], dn, a),
        remote(2, pfx.at[pl.ds(1, 1)], pfx.at[pl.ds(17, 1)], dn, a),
        remote(2, stage.at[pl.ds(128, 16)], hc.at[pl.ds(128, 16)], dn, a_up),
        remote(2, stage.at[pl.ds(144, 16)], hc.at[pl.ds(144, 16)], dn, a_dn),
    ]
    sides = [
        remote(0, stage.at[pl.ds(0, 48)], hc.at[pl.ds(0, 48)], d, a_up),
        remote(0, stage.at[pl.ds(48, 48)], hc.at[pl.ds(48, 48)], d, a_dn),
    ]
    for copy in sides:
        copy.start()

    @pl.when(d < ND - 1)
    def _():
        for copy in to_up:
            copy.start()

    @pl.when(d > 0)
    def _():
        for copy in to_dn:
            copy.start()

    def drain(sem, rows):
        view = w2.at[0, pl.ds(0, rows)]
        pltpu.make_async_copy(view, view, sem).wait()

    build_mixers()
    build_resample()

    row16 = lax.broadcasted_iota(jnp.int32, (16, RC), 0)
    is0, is1, is14, is15 = (row16 == n for n in (0, 1, 14, 15))
    row64 = lax.broadcasted_iota(jnp.int32, (NW, RC), 0)

    def build_s1(e, carry):
        x = g2x[e].astype(F32)
        ahead = pltpu.roll(x, NW - 1, 0)
        behind = pltpu.roll(x, 1, 0)
        s1[e, :, 0:RC] = jnp.where(row64 == NW - 1, 0.0, ahead).astype(BF16)
        s1[e, :, RC : 2 * RC] = g2x[e]
        s1[e, :, 2 * RC :] = jnp.where(row64 == 0, 0.0, behind).astype(BF16)
        t1[e, :, 0:RC] = jnp.where(is1, behind[0:16], 0.0).astype(BF16)
        t1[e, :, 2 * RC :] = jnp.where(is14, ahead[48:64], 0.0).astype(BF16)
        return carry

    def joined(rows, w):
        total = 0.0
        for td in range(3):
            total = total + jnp.dot(
                rows[td], w[3 * td : 3 * td + 3].reshape(3 * RC, RC), preferred_element_type=F32
            )
        return total

    def gated(f, h):
        x = jnp.where(pfx[f].astype(F32) > 0, h, 0.0)
        s2[f, :, 0:RC] = pltpu.roll(x, NW - 1, 0).astype(BF16)
        s2[f, :, RC : 2 * RC] = x.astype(BF16)
        s2[f, :, 2 * RC :] = pltpu.roll(x, 1, 0).astype(BF16)

    def conv1(chunk, carry):
        base = 2 + chunk * CH1
        rows = [s1[pl.ds(base + 2 - td, CH1)].reshape(CH1 * NW, 3 * RC) for td in range(3)]
        total = joined(rows, w2).reshape(CH1, NW, RC)
        for n in range(CH1):
            hidden[base + n, 0:16] = total[n, 0:16]
            hidden[base + n, 16:32] = total[n, 48:64]
            gated(base + n, total[n])
        return carry

    lax.fori_loop(2, 18, build_s1, 0, unroll=2)
    lax.fori_loop(0, 14 // CH1, conv1, 0)

    ld_exp.wait()
    drain(fr_sem.at[0], 96)

    @pl.when(d < ND - 1)
    def _():
        drain(fr_sem.at[2], 224)

    @pl.when(d > 0)
    def _():
        drain(fr_sem.at[1], 224)

    edges[...] = jnp.dot(expm[...], hc[...], preferred_element_type=F32)
    for e in (0, 1, 18, 19):
        build_s1(e, 0)

    def add_edges(e, carry):
        tile = [edges[pl.ds(pl.multiple_of((20 * n + e) * 16, 16), 16)].astype(BF16) for n in range(3)]
        t1[e, :, 0:RC] = t1[e, :, 0:RC] + tile[0]
        t1[e, :, RC : 2 * RC] = tile[1]
        t1[e, :, 2 * RC :] = t1[e, :, 2 * RC :] + tile[2]
        return carry

    lax.fori_loop(0, 20, add_edges, 0, unroll=4)
    fix[...] = joined(
        [t1[2 - td : 20 - td].reshape(18 * 16, 3 * RC) for td in range(3)], w2
    ).reshape(18, 16, RC)
    for f in (0, 16):
        total = joined(
            [s1[f + 2 - td : f + 4 - td].reshape(2 * NW, 3 * RC) for td in range(3)], w2
        ).reshape(2, NW, RC)
        for n in range(2):
            hidden[f + n, 0:16] = total[n, 0:16]
            hidden[f + n, 16:32] = total[n, 48:64]
            gated(f + n, total[n])

    def build_s2(f, carry):
        c = fix[f]
        left = jnp.where(is0, hidden[f, 0:16] + c, hidden[f, 0:16])
        right = jnp.where(is15, hidden[f, 16:32] + c, hidden[f, 16:32])
        left = jnp.where(pfx[f, 0:16].astype(F32) > 0, left, 0.0)
        right = jnp.where(pfx[f, 48:64].astype(F32) > 0, right, 0.0)
        gate = edges[pl.ds(pl.multiple_of((60 + f) * 16, 16), 16)]
        side = jnp.where(gate > 0, c, 0.0)
        s2[f, 0:16, RC : 2 * RC] = left.astype(BF16)
        s2[f, 48:64, RC : 2 * RC] = right.astype(BF16)
        s2[f, 48:64, 0:RC] = jnp.where(is15, pltpu.roll(side, 1, 0), pltpu.roll(right, 15, 0)).astype(BF16)
        s2[f, 0:16, 2 * RC :] = jnp.where(is0, pltpu.roll(side, 15, 0), pltpu.roll(left, 1, 0)).astype(BF16)
        return carry

    lax.fori_loop(0, 18, build_s2, 0, unroll=US2)

    def conv2(chunk, carry):
        base = chunk * CH2
        rows = [s2[pl.ds(base + 2 - td, CH2)].reshape(CH2 * NW, 3 * RC) for td in range(3)]
        total = joined(rows, w1)
        vol[pl.ds(base, CH2)] = total.astype(BF16).reshape(CH2, NW, RC)
        return carry

    lax.fori_loop(0, NS // CH2, conv2, 0, unroll=True)

    def mix(s, carry):
        v = jnp.concatenate([vol[s, :, 0:128], vol[s, :, 128:256]], axis=0)
        y = jnp.dot(v, rt[s], preferred_element_type=F32).astype(BF16)
        for k in range(CAMS):
            ymix[k, s, :, 0:128] = y[0:64, k * 128 : k * 128 + 128]
            ymix[k, s, :, 128:256] = y[64:128, k * 128 : k * 128 + 128]
        return carry

    lax.fori_loop(0, NS, mix, 0, unroll=True)

    block = lax.broadcasted_iota(jnp.int32, (1, 16, 128), 2) // 16

    def back(j, src_row, rows, dst_row, col):
        pltpu.make_async_remote_copy(
            src_ref=zbuf.at[j, pl.ds(src_row, rows)],
            dst_ref=rbuf.at[pl.ds(j * 128 + dst_row, rows)],
            send_sem=bs_sem, recv_sem=br_sem,
            device_id={"depth": lax.rem(d + j, ND), "azim": col},
            device_id_type=pl.DeviceIdType.MESH,
        ).start()

    order = list(range(1, ND)) + [0]
    slots = [
        lax.rem(block - lax.rem(d + j, ND) + ND, ND).astype(F32).astype(BF16) for j in range(ND)
    ]
    for part in range(2):
        source = []
        for k in range(CAMS):
            cam = jnp.dot(
                band[k, part * 64 : part * 64 + 64], ymix[k].reshape(NS * NW, RC),
                preferred_element_type=F32,
            )
            source.append(cam[:, 0:128].astype(BF16).reshape(4, 16, 128))
            source.append(pltpu.roll(cam[:, 128:256], 16, 1).astype(BF16).reshape(4, 16, 128))
        for j in order:
            z = source[0]
            for q in range(1, ROWS):
                z = jnp.where(slots[j] == jnp.asarray(q, BF16), source[q], z)
            if part == 1 and j == 0:
                rbuf[0:64] = z.reshape(64, 128)
                continue
            zbuf[j, part * 64 : part * 64 + 64] = z.reshape(64, 128)
            if part == 0:
                back(j, 0, 32, 64, a_up)
                back(j, 32, 32, 96, a_dn)
            else:
                back(j, 64, 64, 0, a)

    arrived = rbuf.at[pl.ds(64, ND * 128 - 64)]
    pltpu.make_async_copy(arrived, arrived, br_sem).wait()
    total = jnp.zeros((NW, 128), F32)
    for j in range(ND):
        own = rbuf[j * 128 : j * 128 + 64].astype(F32)
        total = total + (own + rbuf[j * 128 + 64 : j * 128 + 128].astype(F32))
    out_ref[0] = pltpu.roll(total, lax.rem(ND - d, ND) * 16, 1)

    pltpu.make_async_copy(arrived, arrived, bs_sem).wait()
    drain(fs_sem.at[0], 96)

    @pl.when(d < ND - 1)
    def _():
        drain(fs_sem.at[1], 224)

    @pl.when(d > 0)
    def _():
        drain(fs_sem.at[2], 224)


def body(cotangent, pre_second, pre_first, kernel_first, kernel_second, row_resample, col_taps, band_width, col_offset):
    consts = [
        jnp.asarray(x, BF16)
        for x in (stage_select(), edge_expand(), row_place(), lane_rows())
    ]
    vm = pltpu.VMEM
    scratch = [
        vm((NS, NW, RC), BF16), vm((NS, NW, RC), BF16), vm((18, NW, RC), BF16),
        vm((20, NW, RC), BF16), vm((2, 9, 96, C), BF16), vm((CAMS, ROWS * ROWS, NS), F32),
        vm((CAMS, TAPS, NS), F32), vm((CAMS, NS), jnp.int32), vm((CAMS, NS), jnp.int32),
        vm((160, 1024), BF16), vm((78 * 16, 160), BF16), vm((2, ROWS, 96, RC), BF16),
        vm((CAMS, ROWS * ROWS, 128), BF16), vm((CAMS, NS, 128), F32),
        vm((160, RC), BF16), vm((160, RC), BF16),
        vm((20, NW, 3 * RC), BF16), vm((20, 16, 3 * RC), BF16), vm((18, NW, 3 * RC), BF16),
        vm((18, 32, RC), F32), vm((18, 16, RC), F32), vm((78 * 16, RC), F32), vm((2, 288, 96), BF16),
        vm((9, RC, RC), BF16), vm((9, RC, RC), BF16),
        vm((CAMS * NS * ROWS, 128), F32), vm((NS, 128, CAMS * 128), BF16),
        vm((CAMS, 128, NS * NW), BF16), vm((NS, NW, RC), BF16), vm((CAMS, NS, NW, RC), BF16),
        vm((ROWS, 128, 128), BF16), vm((ND * 128, 128), BF16),
        pltpu.SemaphoreType.DMA((13 + 2 * PARTS,)), pltpu.SemaphoreType.DMA((3,)),
        pltpu.SemaphoreType.DMA((3,)), pltpu.SemaphoreType.DMA, pltpu.SemaphoreType.DMA,
    ]
    return pl.pallas_call(
        kernel,
        out_shape=jax.ShapeDtypeStruct((1, NW, 128), F32),
        in_specs=[pl.BlockSpec(memory_space=pl.ANY)] * 13,
        out_specs=pl.BlockSpec(memory_space=pltpu.VMEM),
        scratch_shapes=scratch,
        compiler_params=pltpu.CompilerParams(
            collective_id=0, has_side_effects=True, vmem_limit_bytes=62 * 1024 * 1024
        ),
    )(
        cotangent, pre_second, pre_first,
        kernel_first.reshape(9, 96, C), kernel_second.reshape(9, 96, C),
        row_resample.transpose(0, 2, 3, 1).reshape(CAMS, ROWS * ROWS, NS), col_taps.transpose(0, 2, 1),
        band_width, col_offset, *consts,
    )


def solution(mesh):
    placed = (
        P("depth", "azim", None),
        P("depth", "azim", None),
        P("depth", "azim", None),
        P(),
        P(),
        P(None, "depth", None, None),
        P(None, "depth", None),
        P(None, "depth"),
        P(None, "depth"),
    )
    return jax.shard_map(
        body, mesh=mesh, in_specs=placed, out_specs=P("depth", "azim", None), check_vma=False
    )
```
